32 devices in a mesh: grp: 2 (over x), bas: 4 (over y, core), aux: 4 (over z).
Axes of the slice: x: 2, y: 2, z: 4, core: 2. Of those that a mesh axis runs over, the one named last changes fastest.
Arguments:
- three_index: bfloat16 [64, 512, 384], P(('grp', 'aux'), 'bas'), parts along dimension 0, may hold values from -6 to 6
- screen: int32 [8, 3], P(('grp', 'bas')), parts along dimension 0, may hold values 0 or 1
- green_occ: bfloat16 [1024, 512], P(('grp', 'bas')), parts along dimension 0, as said below
- green_virt: bfloat16 [1024, 512], P(('grp', 'bas')), parts along dimension 0, as said below
Outputs:
- chi: float32 [64, 32], P(('grp', 'aux'), 'bas'), parts along dimension 0
The draws below stay inside these ranges and needn't reach their ends.
There are 2 independent parts, one for each index of `grp`. The reference program is written for one: setup_inputs(seed, part) draws one part's arguments, and reference() takes and returns one part's arrays. A program takes and returns all parts, laid end to end along the dimension named above; each array names one. Nothing has to cross between parts.
Inputs may be any that keep to these rules, and one draw needn't show every extreme that they name: `green_occ`: symmetric matrix. `green_virt`: symmetric matrix.
All inputs are finite; a program needn't handle non-finite values. No bound on the sum of `screen` on one device may be relied on, other than what follows from the above.
Results may differ from the reference program's by a relative error of at most 0.0041.
Values may be sent and summed in bfloat16 or wider, within the bound.
A program may use at most 128 MiB of HBM per device.

```python
import math
import jax
import jax.numpy as jnp
from jax import lax

BLK = 128
NBASIS = 512
NAUX = 32


def symmetric_green(key, power):
    uniform_part = jax.random.uniform(key, (NBASIS, NBASIS), jnp.float32, -1.0, 1.0)
    shaped = jnp.sign(uniform_part) * jnp.abs(uniform_part) ** power
    return ((shaped + shaped.T) * (1.5 / NBASIS) ** 0.5).astype(jnp.bfloat16)


def draw_green_occ(key, part):
    key = jax.random.fold_in(key, 11)
    return symmetric_green(key, 1.0)


def draw_green_virt(key, part):
    key = jax.random.fold_in(key, 23)
    return symmetric_green(key, 1.0)


def place_ends(entries, key, smallest, top_value):
    extent = entries.shape
    spot = [jax.random.randint(jax.random.fold_in(key, axis), (), 0, extent[axis]) for axis in range(len(extent))]
    entries = entries.at[tuple(spot)].set(smallest)
    longest = extent.index(max(extent))
    spot[longest] = (spot[longest] + 1) % extent[longest]
    return entries.at[tuple(spot)].set(top_value)


def level_of(rng, dims, shards, smallest, top_value):
    level, own = 1.0, jax.random.fold_in(rng, 6)
    for axis_at, blocks in shards:
        draws = jnp.exp(jax.random.uniform(jax.random.fold_in(own, axis_at), (blocks,), jnp.float32, smallest / len(shards), top_value / len(shards)))
        level = level * jnp.repeat(draws, dims[axis_at] // blocks).reshape([-1 if axis == axis_at else 1 for axis in range(len(dims))])
    return level


def noise(own_key, shape, deviation, reach, pieces=(), dtype=jnp.bfloat16):
    level = level_of(own_key, shape, pieces, -0.22, 0.18) if pieces else 1.0
    values = jax.random.normal(own_key, shape, jnp.float32) * deviation * level
    return jnp.minimum(jnp.maximum(values, -reach), reach).astype(dtype)


def setup_inputs(seed: int = 0, part: int = 0) -> dict:
    streams_of = jax.random.split(jax.random.key(seed), 5)
    own_keys = jax.random.split(jax.random.fold_in(streams_of[4], part), 5)
    return {
        "three_index": noise(own_keys[0], (NAUX, NBASIS, 3 * BLK), 1.0, 6.0, ((0, 4), (1, 4))),
        "screen": place_ends((jax.random.randint(own_keys[1], (NBASIS // BLK, 3), 0, 4) < 3).astype(jnp.int32), jax.random.fold_in(own_keys[1], 1), 0, 1),
        "green_occ": draw_green_occ(jax.random.fold_in(jax.random.fold_in(streams_of[4], part), 71), part),
        "green_virt": draw_green_virt(jax.random.fold_in(jax.random.fold_in(streams_of[4], part), 71), part),
    }


def reference(three_index, screen, green_occ, green_virt):
    blocks = NBASIS // BLK
    screen_flags = screen.astype(jnp.bfloat16)
    masked = (three_index.reshape(NAUX, blocks, BLK, 3, BLK) * screen_flags[None, :, None, :, None]).reshape(NAUX, NBASIS, 3 * BLK)
    virt_blocks = green_virt.reshape(blocks, BLK, NBASIS).astype(jnp.float32)
    virt_stack = jnp.stack([jnp.roll(virt_blocks, 1, 0), virt_blocks, jnp.roll(virt_blocks, -1, 0)], 1).reshape(blocks, 3 * BLK, NBASIS)
    occ_blocks = green_occ.reshape(blocks, BLK, NBASIS).astype(jnp.float32)

    def per_aux(masked_row):
        half = jnp.einsum('mlc,mcn->mln', masked_row.reshape(blocks, BLK, 3 * BLK).astype(jnp.float32), virt_stack)
        half = half.astype(jnp.bfloat16).reshape(NBASIS, blocks, BLK).astype(jnp.float32)
        band_cols = jnp.stack([jnp.roll(half, 1, 1), half, jnp.roll(half, -1, 1)], 2)
        middle = jnp.einsum('mil,lmwj->miwj', occ_blocks, band_cols)
        return middle.reshape(NBASIS, 3 * BLK).astype(jnp.bfloat16)
    middle = lax.map(per_aux, masked)
    total = jnp.einsum('pmc,qmc->pq', masked.astype(jnp.float32), middle.astype(jnp.float32))
    return total * (-2.0 / math.sqrt(3 * BLK * BLK))
```

```python
import functools
import math

import jax
import jax.numpy as jnp
from jax import lax
from jax.experimental import pallas as pl
from jax.experimental.pallas import tpu as pltpu
from jax.sharding import PartitionSpec as P

MESH = pl.DeviceIdType.MESH
CHUNKS = 4


def kernel(
    scale,
    three_ref, screen_ref, occ_ref, virt_ref, out_ref,
    ball, zall, mid, half, virt_band, virt_ext, part, part_t, chi_in,
    y_send, y_recv, core_send, core_recv, fwd_send, fwd_recv,
    virt_send, virt_recv, z_send, z_recv, chi_send, chi_recv,
):
    aux_rows, width, band = three_ref.shape
    blocks = 4
    step = aux_rows // CHUNKS
    g, b, z = lax.axis_index("grp"), lax.axis_index("bas"), lax.axis_index("aux")
    core = b + 1 - 2 * lax.rem(b, 2)
    across = lax.rem(b + 2, blocks)
    corner = blocks - 1 - b
    above, below = lax.rem(b + 1, blocks), lax.rem(b + blocks - 1, blocks)

    barrier = pltpu.get_barrier_semaphore()
    for k in range(1, 16):
        other = lax.rem(b * 4 + z + k, 16)
        pl.semaphore_signal(
            barrier, inc=1, device_id=(g, other // 4, lax.rem(other, 4)), device_id_type=MESH
        )

    for w in range(3):
        flag = jnp.full((width, width), screen_ref[0, w].astype(jnp.float32)).astype(jnp.bfloat16)
        cols = pl.ds(w * width, width)
        for q in range(aux_rows):
            value = three_ref[q, :, cols] * flag
            ball[b, q, :, cols] = value
            zall[z, q, :, cols] = value
    pl.semaphore_wait(barrier, 15)

    def remote(src, dst, send, recv, bas, aux):
        return pltpu.make_async_remote_copy(
            src_ref=src, dst_ref=dst, send_sem=send, recv_sem=recv,
            device_id=(g, bas, aux), device_id_type=MESH,
        )

    def bas_copy(block, k, sends, recvs, to):
        rows = ball.at[block, pl.ds(k * step, step)]
        return remote(rows, rows, sends.at[k], recvs.at[k], to, z)

    def z_copy(source, k, to):
        rows = zall.at[source, pl.ds(k * step, step)]
        return remote(rows, rows, z_send.at[source, k], z_recv.at[source, k], b, to)

    z_right, z_left = lax.rem(z + 1, 4), lax.rem(z + 3, 4)

    virt_up = remote(virt_ref, virt_band.at[0], virt_send.at[0], virt_recv.at[0], above, z)
    virt_down = remote(virt_ref, virt_band.at[2], virt_send.at[1], virt_recv.at[1], below, z)
    virt_up.start()
    virt_down.start()
    for k in range(CHUNKS):
        bas_copy(b, k, y_send, y_recv, across).start()
        for s in (0, 1):
            @pl.when(z == s)
            def _():
                z_copy(s, k, z_right).start()

        @pl.when(z == 3)
        def _():
            z_copy(3, k, z_left).start()
        bas_copy(b, k, core_send, core_recv, core).start()

    virt_band[1] = virt_ref[...]
    virt_up.wait_recv()
    virt_down.wait_recv()
    for w in range(3):
        turned = virt_band[w].astype(jnp.float32).T.astype(jnp.bfloat16)
        cols = pl.ds(w * width, width)
        virt_ext[pl.ds(width, blocks * width), cols] = turned
        virt_ext[pl.ds(0, width), cols] = turned[(blocks - 1) * width :]
        virt_ext[pl.ds((blocks + 1) * width, width), cols] = turned[:width]

    def middle_of(k):
        bas_copy(core, k, core_send, core_recv, core).wait_recv()
        bas_copy(corner, k, fwd_send, fwd_recv, core).wait_recv()

        def one_block(l, carry):
            rows = pl.ds(pl.multiple_of(l * width, width), width)
            virt = virt_ext[pl.ds(pl.multiple_of(l * width, width), band), :]
            three = ball[l, pl.ds(k * step, step)].reshape(step * width, band)
            value = jnp.dot(three, virt, preferred_element_type=jnp.float32)
            half[:, rows, :] = value.astype(jnp.bfloat16).reshape(step, width, band)
            return carry

        lax.fori_loop(0, blocks, one_block, 0)
        for q in range(step):
            mid[k * step + q] = jnp.dot(
                occ_ref[...], half[q], preferred_element_type=jnp.float32
            ).astype(jnp.bfloat16)

    for k in range(CHUNKS):
        bas_copy(across, k, y_send, y_recv, across).wait_recv()
        bas_copy(across, k, fwd_send, fwd_recv, core).start()

        @pl.when(z == 1)
        def _():
            z_copy(0, k, z_right).wait_recv()
            z_copy(0, k, z_right).start()

        @pl.when(z == 2)
        def _():
            z_copy(1, k, z_right).wait_recv()
            z_copy(1, k, z_right).start()

        if k:
            middle_of(k - 1)
    middle_of(CHUNKS - 1)

    row = lax.broadcasted_iota(jnp.int32, (width, 2 * width), 0)
    col = lax.broadcasted_iota(jnp.int32, (width, 2 * width), 1)
    same = jnp.where((col == row) | (col == row + width), 1.0, 0.0).astype(jnp.float32)
    lane = lax.broadcasted_iota(jnp.int32, (aux_rows, 128), 1)

    def chi_copy(i, turned):
        src = part_t.at[i] if turned else part.at[i]
        return remote(
            src, chi_in.at[b], chi_send.at[i, int(turned)], chi_recv.at[b],
            i if turned else z, z if turned else i,
        )

    def pair(i):
        def two(t, acc):
            rows = zall[i].reshape(aux_rows * width, band)
            ours = mid[pl.ds(2 * t, 2)].reshape(2 * width, band)
            prod = lax.dot_general(
                rows, ours, (((1,), (1,)), ((), ())), preferred_element_type=jnp.float32
            )
            kept = jnp.sum(prod.reshape(aux_rows, width, 2 * width) * same[None], axis=1)
            first = jnp.sum(kept[:, :width], axis=1, keepdims=True)
            second = jnp.sum(kept[:, width:], axis=1, keepdims=True)
            return jnp.where(lane == 2 * t, first, jnp.where(lane == 2 * t + 1, second, acc))

        acc = lax.fori_loop(0, aux_rows // 2, two, jnp.zeros((aux_rows, 128), jnp.float32))
        return acc

    def cross(i):
        acc = pair(i)
        part[i] = acc
        full = jnp.concatenate([acc, jnp.zeros((128 - aux_rows, 128), jnp.float32)], 0)
        part_t[i] = full.T[:aux_rows]
        chi_copy(i, False).start()

        @pl.when(b == i)
        def _():
            chi_in[b] = part_t[i]

        @pl.when(b != i)
        def _():
            chi_copy(i, True).start()

    def relay(k):
        @pl.when(z == 2)
        def _():
            z_copy(0, k, z_right).wait_recv()
            z_copy(0, k, z_right).start()

    relay(0)
    part[z] = pair(z)
    own = remote(part.at[z], chi_in.at[b], chi_send.at[z, 0], chi_recv.at[b], z, z)

    @pl.when(b == z)
    def _():
        chi_in[b] = part[z]

    @pl.when(b != z)
    def _():
        own.start()

    relay(1)

    @pl.when(z >= 2)
    def _():
        @pl.when(z == 3)
        def _():
            for k in range(CHUNKS):
                z_copy(1, k, z_right).wait_recv()
        cross(1)

    relay(2)

    @pl.when(z == 2)
    def _():
        for k in range(CHUNKS):
            z_copy(3, k, z_left).wait_recv()
        cross(3)

    relay(3)

    @pl.when(z >= 1)
    def _():
        @pl.when(z == 3)
        def _():
            for k in range(CHUNKS):
                z_copy(0, k, z_right).wait_recv()
        cross(0)

    both = jnp.maximum(b, z)
    least = jnp.minimum(b, z)
    owner = jnp.where((both == 3) & (least == 2), 2, both)
    for k in range(blocks):
        @pl.when((b != k) | (owner != z))
        def _():
            remote(part.at[0], chi_in.at[k], chi_send.at[0, 0], chi_recv.at[k], b, z_right).wait_recv()
    total = chi_in[0] + chi_in[1] + chi_in[2] + chi_in[3]
    out_ref[...] = total[:, : out_ref.shape[1]] * scale

    virt_up.wait_send()
    virt_down.wait_send()
    for k in range(CHUNKS):
        bas_copy(b, k, y_send, y_recv, across).wait_send()
        bas_copy(b, k, core_send, core_recv, core).wait_send()
        bas_copy(across, k, fwd_send, fwd_recv, core).wait_send()

        @pl.when(z <= 2)
        def _():
            z_copy(0, k, z_right).wait_send()

        @pl.when((z == 1) | (z == 2))
        def _():
            z_copy(1, k, z_right).wait_send()

        @pl.when(z == 3)
        def _():
            z_copy(3, k, z_left).wait_send()

    @pl.when(b != z)
    def _():
        own.wait_send()

    def cross_sent(i):
        chi_copy(i, False).wait_send()

        @pl.when(b != i)
        def _():
            chi_copy(i, True).wait_send()

    @pl.when(z >= 1)
    def _():
        cross_sent(0)

    @pl.when(z >= 2)
    def _():
        cross_sent(1)

    @pl.when(z == 2)
    def _():
        cross_sent(3)


def one_kernel(three_index, screen, green_occ, green_virt):
    aux_rows, width, band = three_index.shape
    nbasis = green_virt.shape[1]
    scale = -2.0 / math.sqrt(3 * width * width)
    bf16, f32 = jnp.bfloat16, jnp.float32
    dma = pltpu.SemaphoreType.DMA
    vmem = pl.BlockSpec(memory_space=pltpu.VMEM)
    return pl.pallas_call(
        functools.partial(kernel, scale),
        out_shape=jax.ShapeDtypeStruct((aux_rows, aux_rows), f32),
        in_specs=[vmem, pl.BlockSpec(memory_space=pltpu.SMEM), vmem, vmem],
        out_specs=vmem,
        scratch_shapes=[
            pltpu.VMEM((4, aux_rows, width, band), bf16),
            pltpu.VMEM((4, aux_rows, width, band), bf16),
            pltpu.VMEM((aux_rows, width, band), bf16),
            pltpu.VMEM((aux_rows // CHUNKS, nbasis, band), bf16),
            pltpu.VMEM((3, width, nbasis), bf16),
            pltpu.VMEM((nbasis + 2 * width, band), bf16),
            pltpu.VMEM((4, aux_rows, 128), f32),
            pltpu.VMEM((4, aux_rows, 128), f32),
            pltpu.VMEM((4, aux_rows, 128), f32),
        ]
        + [dma((CHUNKS,))] * 6
        + [dma((2,))] * 2
        + [dma((4, CHUNKS))] * 2
        + [dma((4, 2)), dma((4,))],
        compiler_params=pltpu.CompilerParams(
            collective_id=0, has_side_effects=True, vmem_limit_bytes=40 * 1024 * 1024
        ),
    )(three_index, screen, green_occ, green_virt)


def padded_2(x, sides, width):
    for axis, dim in sides:
        count, length = (lax.axis_size(axis), x.shape[dim])
        up = [(i, (i + 1) % count) for i in range(count)]
        down = [(j, i) for i, j in up]
        last = lax.slice_in_dim(x, length - width, length, axis=dim)
        initial = lax.slice_in_dim(x, 0, width, axis=dim)
        before = lax.ppermute(last, axis, up)
        after = lax.ppermute(initial, axis, down)
        x = jnp.concatenate([before, x, after], axis=dim)
    return x


def body(three_index, screen, green_occ, green_virt):
    width = green_virt.shape[0]
    aux_rows = three_index.shape[0]
    nbasis = green_virt.shape[1]
    screen_flags = screen[0].astype(jnp.bfloat16)
    masked = (
        three_index.reshape(aux_rows, width, 3, width) * screen_flags[None, None, :, None]
    ).reshape(aux_rows, width, 3 * width)
    virt_rows = padded_2(green_virt, (("bas", 0),), width)
    half = jnp.dot(
        masked.reshape(aux_rows * width, 3 * width), virt_rows, preferred_element_type=jnp.float32
    )
    half = half.astype(jnp.bfloat16).reshape(aux_rows, width, nbasis)
    padded = jnp.concatenate([half[:, :, nbasis - width :], half, half[:, :, :width]], 2)

    def one_block(offset):
        begin = offset * width
        occ_cols = lax.dynamic_slice_in_dim(green_occ, begin, width, 1)
        virt_band = lax.dynamic_slice_in_dim(padded, begin, 3 * width, 2)
        return jnp.einsum("lm,alc->mac", occ_cols, virt_band, preferred_element_type=jnp.float32)

    parts_out = lax.map(
        one_block, jnp.arange(lax.axis_size("bas") * width // width, dtype=jnp.int32)
    )
    summed = lax.psum_scatter(
        parts_out.reshape(lax.axis_size("bas") * width, aux_rows, 3 * width),
        "bas",
        scatter_dimension=0,
        tiled=True,
    )
    middle = jnp.transpose(summed, (1, 0, 2)).astype(jnp.bfloat16)
    partial_chi = jnp.einsum(
        "pmc,qmc->pq",
        masked,
        lax.all_gather(middle, "aux", axis=0, tiled=True),
        preferred_element_type=jnp.float32,
    )
    summed_chi = lax.psum_scatter(partial_chi, "bas", scatter_dimension=1, tiled=True)
    return summed_chi * (-2.0 / math.sqrt(3 * width * width))


def solution(mesh):
    in_specs = (
        P(("grp", "aux"), "bas", None),
        P(("grp", "bas"), None),
        P(("grp", "bas"), None),
        P(("grp", "bas"), None),
    )
    out_specs = P(("grp", "aux"), "bas")
    fits = mesh.shape["bas"] == 4 and mesh.shape["aux"] == 4
    return jax.shard_map(one_kernel if fits else body, mesh=mesh, in_specs=in_specs, out_specs=out_specs, check_vma=False)
```

```python
import functools
import math

import jax
import jax.numpy as jnp
from jax import lax
from jax.experimental import pallas as pl
from jax.experimental.pallas import tpu as pltpu
from jax.sharding import PartitionSpec as P

MESH = pl.DeviceIdType.MESH
CHUNKS = 4


def kernel(
    scale,
    three_ref, screen_ref, occ_hbm, virt_hbm, out_ref,
    ball, zall, mall, mid, half, occ_ref, virt_band, virt_ext, flags_ref, part, part_t, chi_in,
    y_send, y_recv, core_send, core_recv, fwd_send, fwd_recv,
    virt_send, virt_recv, z_send, z_recv, chi_send, chi_recv, local_sem,
):
    aux_rows, width, band = three_ref.shape
    blocks = 4
    step = aux_rows // CHUNKS
    late = 3 * width // 8
    early = width - late
    g, b, z = lax.axis_index("grp"), lax.axis_index("bas"), lax.axis_index("aux")
    core = b + 1 - 2 * lax.rem(b, 2)
    across = lax.rem(b + 2, blocks)
    corner = blocks - 1 - b
    above, below = lax.rem(b + 1, blocks), lax.rem(b + blocks - 1, blocks)

    barrier = pltpu.get_barrier_semaphore()
    for k in range(1, 16):
        other = lax.rem(b * 4 + z + k, 16)
        pl.semaphore_signal(
            barrier, inc=1, device_id=(g, other // 4, lax.rem(other, 4)), device_id_type=MESH
        )

    own_copies = [
        pltpu.make_async_copy(screen_ref, flags_ref, local_sem.at[0]),
        pltpu.make_async_copy(three_ref, ball.at[b], local_sem.at[1]),
        pltpu.make_async_copy(virt_hbm, virt_band.at[1], local_sem.at[2]),
        pltpu.make_async_copy(occ_hbm, occ_ref, local_sem.at[3]),
    ]
    for copy in own_copies:
        copy.start()
    own_copies[0].wait()
    own_copies[1].wait()
    lane = lax.broadcasted_iota(jnp.int32, (1, band), 1)
    flags = [flags_ref[0, w].astype(jnp.float32) for w in range(3)]
    flag_row = jnp.where(lane < width, flags[0], jnp.where(lane < 2 * width, flags[1], flags[2]))
    for w in range(3):
        flag = jnp.full((width, width), flags[w]).astype(jnp.bfloat16)
        cols = pl.ds(w * width, width)
        for q in range(aux_rows):
            ball[b, q, :, cols] = ball[b, q, :, cols] * flag
    pl.semaphore_wait(barrier, 15)

    def remote(src, dst, send, recv, bas, aux):
        return pltpu.make_async_remote_copy(
            src_ref=src, dst_ref=dst, send_sem=send, recv_sem=recv,
            device_id=(g, bas, aux), device_id_type=MESH,
        )

    def bas_copy(block, k, sends, recvs, to):
        rows = ball.at[block, pl.ds(k * step, step)]
        return remote(rows, rows, sends.at[k], recvs.at[k], to, z)

    z_right, z_left = lax.rem(z + 1, 4), lax.rem(z + 3, 4)

    def flow(f, k, first):
        aux = pl.ds(k * step, step)
        if f >= 4:
            dst = mall.at[f - 4, aux]
            src = mid.at[aux, pl.ds(early, late)] if first else dst
        else:
            rows = (pl.ds(0, early), pl.ds(0, early), pl.ds(early, late), pl.ds(0, width))[f]
            dst = zall.at[(0, 1, 0, 3)[f], aux, rows]
            src = three_ref.at[aux, rows] if first else dst
        return remote(src, dst, z_send.at[f, k], z_recv.at[f, k], b, z_right if f < 3 else z_left)

    def relay(at, f, k):
        @pl.when(z == at)
        def _():
            flow(f, k, False).wait_recv()
            flow(f, k, False).start()

    def arrived(f):
        for k in range(CHUNKS):
            flow(f, k, False).wait_recv()

    virt_up = remote(virt_hbm, virt_band.at[0], virt_send.at[0], virt_recv.at[0], above, z)
    virt_down = remote(virt_hbm, virt_band.at[2], virt_send.at[1], virt_recv.at[1], below, z)
    for at, f in ((0, 0), (1, 1), (3, 3)):
        @pl.when(z == at)
        def _():
            for k in range(CHUNKS):
                flow(f, k, True).start()
    virt_up.start()
    virt_down.start()
    for k in range(CHUNKS):
        bas_copy(b, k, y_send, y_recv, across).start()
        bas_copy(b, k, core_send, core_recv, core).start()

    @pl.when(z == 0)
    def _():
        for k in range(CHUNKS):
            flow(2, k, True).start()

    own_copies[2].wait()
    own_copies[3].wait()
    virt_up.wait_recv()
    virt_down.wait_recv()
    for w in range(3):
        turned = virt_band[w].astype(jnp.float32).T.astype(jnp.bfloat16)
        cols = pl.ds(w * width, width)
        virt_ext[pl.ds(width, blocks * width), cols] = turned
        virt_ext[pl.ds(0, width), cols] = turned[(blocks - 1) * width :]
        virt_ext[pl.ds((blocks + 1) * width, width), cols] = turned[:width]

    def middle_of(k):
        bas_copy(core, k, core_send, core_recv, core).wait_recv()
        bas_copy(corner, k, fwd_send, fwd_recv, core).wait_recv()

        def one_block(l, carry):
            rows = pl.ds(pl.multiple_of(l * width, width), width)
            virt = virt_ext[pl.ds(pl.multiple_of(l * width, width), band), :]
            three = ball[l, pl.ds(k * step, step)].reshape(step * width, band)
            value = jnp.dot(three, virt, preferred_element_type=jnp.float32)
            half[:, rows, :] = value.astype(jnp.bfloat16).reshape(step, width, band)
            return carry

        lax.fori_loop(0, blocks, one_block, 0)
        for q in range(step):
            value = jnp.dot(occ_ref[...], half[q], preferred_element_type=jnp.float32)
            mid[k * step + q] = (value * flag_row).astype(jnp.bfloat16)
        for at, f in ((2, 4), (3, 5)):
            @pl.when(z == at)
            def _():
                flow(f, k, True).start()

    for k in range(CHUNKS):
        bas_copy(across, k, y_send, y_recv, across).wait_recv()
        bas_copy(across, k, fwd_send, fwd_recv, core).start()
        relay(1, 0, k)
        relay(2, 1, k)
        if k >= 2:
            relay(2, 0, k - 2)
        if k:
            middle_of(k - 1)
        if k >= 2:
            relay(2, 5, k - 2)
            relay(1, 4, k - 2)
        if k >= 3:
            relay(1, 5, k - 3)
    middle_of(CHUNKS - 1)

    chi_lane = lax.broadcasted_iota(jnp.int32, (aux_rows, 128), 1)

    def pair(three, middle):
        count = three.shape[1]
        row = lax.broadcasted_iota(jnp.int32, (count, 2 * count), 0)
        col = lax.broadcasted_iota(jnp.int32, (count, 2 * count), 1)
        same = jnp.where((col == row) | (col == row + count), 1.0, 0.0).astype(jnp.float32)
        left = lax.broadcasted_iota(jnp.int32, (aux_rows, 2 * count), 1) < count

        def two(t, acc):
            rows = three[...].reshape(aux_rows * count, band)
            ours = middle[pl.ds(2 * t, 2)].reshape(2 * count, band)
            prod = lax.dot_general(
                rows, ours, (((1,), (1,)), ((), ())), preferred_element_type=jnp.float32
            )
            kept = jnp.sum(prod.reshape(aux_rows, count, 2 * count) * same[None], axis=1)
            first = jnp.sum(jnp.where(left, kept, 0.0), axis=1, keepdims=True)
            second = jnp.sum(jnp.where(left, 0.0, kept), axis=1, keepdims=True)
            return jnp.where(chi_lane == 2 * t, first, jnp.where(chi_lane == 2 * t + 1, second, acc))

        return lax.fori_loop(0, aux_rows // 2, two, jnp.zeros((aux_rows, 128), jnp.float32))

    def chi_copy(other, turned, slot):
        src = part_t.at[other] if turned else part.at[other]
        to = (z, other) if turned == bool(slot) else (other, z)
        return remote(
            src, chi_in.at[b, slot], chi_send.at[other, int(turned)], chi_recv.at[b, slot], *to
        )

    def share(other, slot, acc):
        part[other] = acc
        full = jnp.concatenate([acc, jnp.zeros((128 - aux_rows, 128), jnp.float32)], 0)
        part_t[other] = full.T[:aux_rows]
        near = slot == 0
        chi_copy(other, not near, slot).start()

        @pl.when(b == other)
        def _():
            chi_in[b, slot] = part_t[other] if near else part[other]

        @pl.when(b != other)
        def _():
            chi_copy(other, near, slot).start()

    relay(2, 0, 2)
    relay(2, 5, 2)
    relay(1, 4, 2)
    relay(1, 5, 1)
    part[z] = pair(ball.at[b], mid)
    own = remote(part.at[z], chi_in.at[b, 0], chi_send.at[z, 0], chi_recv.at[b, 0], z, z)

    @pl.when(b == z)
    def _():
        chi_in[b, 0] = part[z]

    @pl.when(b != z)
    def _():
        own.start()

    relay(2, 0, 3)
    relay(2, 5, 3)
    relay(1, 4, 3)
    relay(1, 5, 2)

    @pl.when(z == 1)
    def _():
        arrived(2)
        share(0, 0, pair(zall.at[0], mid))

    relay(1, 5, 3)

    @pl.when(z == 2)
    def _():
        arrived(3)
        share(3, 0, pair(zall.at[3], mid))

    @pl.when(z >= 2)
    def _():
        for i in (1, 0):
            @pl.when(z == 3)
            def _():
                arrived(i)
            share(i, 0, pair(zall.at[i, :, pl.ds(0, early)], mid.at[:, pl.ds(0, early)]))

    @pl.when(z <= 1)
    def _():
        for i in (2, 3):
            @pl.when(z == 0)
            def _():
                arrived(i + 2)
            share(i, 1, pair(ball.at[b, :, pl.ds(early, late)], mall.at[i - 2]))

    top = jnp.maximum(b, z)
    low = jnp.minimum(b, z)
    owner = jnp.where((top == 3) & (low == 2), 2, top)
    split = (low <= 1) & (top >= 2)

    def chi_arrived(k, slot):
        remote(
            part.at[0], chi_in.at[k, slot], chi_send.at[0, 0], chi_recv.at[k, slot], b, z_right
        ).wait_recv()

    for k in range(blocks):
        @pl.when((b != k) | (owner != z))
        def _():
            chi_arrived(k, 0)

        @pl.when(split & ((b != k) | (low != z)))
        def _():
            chi_arrived(k, 1)
    total = chi_in[0, 0] + chi_in[1, 0] + chi_in[2, 0] + chi_in[3, 0]
    out_ref[...] = total[:, : out_ref.shape[1]] * scale

    @pl.when(split)
    def _():
        rest = chi_in[0, 1] + chi_in[1, 1] + chi_in[2, 1] + chi_in[3, 1]
        out_ref[...] = (total + rest)[:, : out_ref.shape[1]] * scale

    virt_up.wait_send()
    virt_down.wait_send()
    for k in range(CHUNKS):
        bas_copy(b, k, y_send, y_recv, across).wait_send()
        bas_copy(b, k, core_send, core_recv, core).wait_send()
        bas_copy(across, k, fwd_send, fwd_recv, core).wait_send()
    for at, f, first in (
        (0, 0, True), (1, 0, False), (2, 0, False), (1, 1, True), (2, 1, False), (0, 2, True),
        (3, 3, True), (2, 4, True), (1, 4, False), (3, 5, True), (2, 5, False), (1, 5, False),
    ):
        @pl.when(z == at)
        def _():
            for k in range(CHUNKS):
                flow(f, k, first).wait_send()

    @pl.when(b != z)
    def _():
        own.wait_send()

    def shared(other, slot):
        near = slot == 0
        chi_copy(other, not near, slot).wait_send()

        @pl.when(b != other)
        def _():
            chi_copy(other, near, slot).wait_send()

    for at, other, slot in (
        (0, 2, 1), (0, 3, 1), (1, 0, 0), (1, 2, 1), (1, 3, 1),
        (2, 0, 0), (2, 1, 0), (2, 3, 0), (3, 0, 0), (3, 1, 0),
    ):
        @pl.when(z == at)
        def _():
            shared(other, slot)


def one_kernel(three_index, screen, green_occ, green_virt):
    aux_rows, width, band = three_index.shape
    nbasis = green_virt.shape[1]
    scale = -2.0 / math.sqrt(3 * width * width)
    bf16, f32 = jnp.bfloat16, jnp.float32
    dma = pltpu.SemaphoreType.DMA
    return pl.pallas_call(
        functools.partial(kernel, scale),
        out_shape=jax.ShapeDtypeStruct((aux_rows, aux_rows), f32),
        in_specs=[pl.BlockSpec(memory_space=pl.ANY)] * 4,
        out_specs=pl.BlockSpec(memory_space=pltpu.VMEM),
        scratch_shapes=[
            pltpu.VMEM((4, aux_rows, width, band), bf16),
            pltpu.VMEM((4, aux_rows, width, band), bf16),
            pltpu.VMEM((2, aux_rows, 3 * width // 8, band), bf16),
            pltpu.VMEM((aux_rows, width, band), bf16),
            pltpu.VMEM((aux_rows // CHUNKS, nbasis, band), bf16),
            pltpu.VMEM((width, nbasis), bf16),
            pltpu.VMEM((3, width, nbasis), bf16),
            pltpu.VMEM((nbasis + 2 * width, band), bf16),
            pltpu.SMEM((1, 3), jnp.int32),
            pltpu.VMEM((4, aux_rows, 128), f32),
            pltpu.VMEM((4, aux_rows, 128), f32),
            pltpu.VMEM((4, 2, aux_rows, 128), f32),
        ]
        + [dma((CHUNKS,))] * 6
        + [dma((2,))] * 2
        + [dma((6, CHUNKS))] * 2
        + [dma((4, 2)), dma((4, 2)), dma((4,))],
        compiler_params=pltpu.CompilerParams(
            collective_id=0, has_side_effects=True, vmem_limit_bytes=56 * 1024 * 1024
        ),
    )(three_index, screen, green_occ, green_virt)


def padded_2(x, sides, width):
    for axis, dim in sides:
        count, length = (lax.axis_size(axis), x.shape[dim])
        up = [(i, (i + 1) % count) for i in range(count)]
        down = [(j, i) for i, j in up]
        last = lax.slice_in_dim(x, length - width, length, axis=dim)
        initial = lax.slice_in_dim(x, 0, width, axis=dim)
        before = lax.ppermute(last, axis, up)
        after = lax.ppermute(initial, axis, down)
        x = jnp.concatenate([before, x, after], axis=dim)
    return x


def body(three_index, screen, green_occ, green_virt):
    width = green_virt.shape[0]
    aux_rows = three_index.shape[0]
    nbasis = green_virt.shape[1]
    screen_flags = screen[0].astype(jnp.bfloat16)
    masked = (
        three_index.reshape(aux_rows, width, 3, width) * screen_flags[None, None, :, None]
    ).reshape(aux_rows, width, 3 * width)
    virt_rows = padded_2(green_virt, (("bas", 0),), width)
    half = jnp.dot(
        masked.reshape(aux_rows * width, 3 * width), virt_rows, preferred_element_type=jnp.float32
    )
    half = half.astype(jnp.bfloat16).reshape(aux_rows, width, nbasis)
    padded = jnp.concatenate([half[:, :, nbasis - width :], half, half[:, :, :width]], 2)

    def one_block(offset):
        begin = offset * width
        occ_cols = lax.dynamic_slice_in_dim(green_occ, begin, width, 1)
        virt_band = lax.dynamic_slice_in_dim(padded, begin, 3 * width, 2)
        return jnp.einsum("lm,alc->mac", occ_cols, virt_band, preferred_element_type=jnp.float32)

    parts_out = lax.map(
        one_block, jnp.arange(lax.axis_size("bas") * width // width, dtype=jnp.int32)
    )
    summed = lax.psum_scatter(
        parts_out.reshape(lax.axis_size("bas") * width, aux_rows, 3 * width),
        "bas",
        scatter_dimension=0,
        tiled=True,
    )
    middle = jnp.transpose(summed, (1, 0, 2)).astype(jnp.bfloat16)
    partial_chi = jnp.einsum(
        "pmc,qmc->pq",
        masked,
        lax.all_gather(middle, "aux", axis=0, tiled=True),
        preferred_element_type=jnp.float32,
    )
    summed_chi = lax.psum_scatter(partial_chi, "bas", scatter_dimension=1, tiled=True)
    return summed_chi * (-2.0 / math.sqrt(3 * width * width))


def solution(mesh):
    in_specs = (
        P(("grp", "aux"), "bas", None),
        P(("grp", "bas"), None),
        P(("grp", "bas"), None),
        P(("grp", "bas"), None),
    )
    out_specs = P(("grp", "aux"), "bas")
    fits = mesh.shape["bas"] == 4 and mesh.shape["aux"] == 4
    return jax.shard_map(one_kernel if fits else body, mesh=mesh, in_specs=in_specs, out_specs=out_specs, check_vma=False)
```

```python
import functools
import math

import jax
import jax.numpy as jnp
from jax import lax
from jax.experimental import pallas as pl
from jax.experimental.pallas import tpu as pltpu
from jax.sharding import PartitionSpec as P

MESH = pl.DeviceIdType.MESH
CHUNKS = 4


def kernel(
    scale,
    three_ref, screen_ref, occ_hbm, virt_hbm, out_ref,
    ball, zall, mall, mid, half, occ_ref, virt_band, virt_ext, flags_ref, flag_rows, part, part_t, chi_in,
    y_send, y_recv, core_send, core_recv, fwd_send, fwd_recv,
    virt_send, virt_recv, z_send, z_recv, chi_send, chi_recv, flag_send, flag_recv, local_sem,
):
    aux_rows, width, band = three_ref.shape
    blocks = 4
    step = aux_rows // CHUNKS
    late = 3 * width // 8
    early = width - late
    g, b, z = lax.axis_index("grp"), lax.axis_index("bas"), lax.axis_index("aux")
    core = b + 1 - 2 * lax.rem(b, 2)
    across = lax.rem(b + 2, blocks)
    corner = blocks - 1 - b
    above, below = lax.rem(b + 1, blocks), lax.rem(b + blocks - 1, blocks)

    barrier = pltpu.get_barrier_semaphore()
    for k in range(1, 16):
        other = lax.rem(b * 4 + z + k, 16)
        pl.semaphore_signal(
            barrier, inc=1, device_id=(g, other // 4, lax.rem(other, 4)), device_id_type=MESH
        )

    own_copies = [
        pltpu.make_async_copy(screen_ref, flags_ref, local_sem.at[0]),
        pltpu.make_async_copy(three_ref, ball.at[b], local_sem.at[1]),
        pltpu.make_async_copy(virt_hbm, virt_band.at[1], local_sem.at[2]),
        pltpu.make_async_copy(occ_hbm, occ_ref, local_sem.at[3]),
    ]
    for copy in own_copies:
        copy.start()
    own_copies[0].wait()
    lane = lax.broadcasted_iota(jnp.int32, (8, band), 1)
    flags = [flags_ref[0, w].astype(jnp.float32) for w in range(3)]
    flag_rows[b] = jnp.where(lane < width, flags[0], jnp.where(lane < 2 * width, flags[1], flags[2]))
    pl.semaphore_wait(barrier, 15)

    def remote(src, dst, send, recv, bas, aux):
        return pltpu.make_async_remote_copy(
            src_ref=src, dst_ref=dst, send_sem=send, recv_sem=recv,
            device_id=(g, bas, aux), device_id_type=MESH,
        )

    def bas_copy(block, k, sends, recvs, to, first=False):
        rows = ball.at[block, pl.ds(k * step, step)]
        src = three_ref.at[pl.ds(k * step, step)] if first else rows
        return remote(src, rows, sends.at[k], recvs.at[k], to, z)

    z_right, z_left = lax.rem(z + 1, 4), lax.rem(z + 3, 4)

    def flow(f, k, first):
        aux = pl.ds(k * step, step)
        if f >= 4:
            dst = mall.at[f - 4, aux]
            src = mid.at[aux, pl.ds(early, late)] if first else dst
        else:
            rows = (pl.ds(0, early), pl.ds(0, early), pl.ds(early, late), pl.ds(0, width))[f]
            dst = zall.at[(0, 1, 0, 3)[f], aux, rows]
            src = three_ref.at[aux, rows] if first else dst
        return remote(src, dst, z_send.at[f, k], z_recv.at[f, k], b, z_right if f < 3 else z_left)

    def relay(at, f, k):
        @pl.when(z == at)
        def _():
            flow(f, k, False).wait_recv()
            flow(f, k, False).start()

    def arrived(f):
        for k in range(CHUNKS):
            flow(f, k, False).wait_recv()

    virt_up = remote(virt_hbm, virt_band.at[0], virt_send.at[0], virt_recv.at[0], above, z)
    virt_down = remote(virt_hbm, virt_band.at[2], virt_send.at[1], virt_recv.at[1], below, z)
    for at, f in ((0, 0), (1, 1), (3, 3)):
        @pl.when(z == at)
        def _():
            for k in range(CHUNKS):
                flow(f, k, True).start()
    virt_up.start()
    virt_down.start()
    flag_copies = [
        remote(flag_rows.at[b], flag_rows.at[b], flag_send.at[n], flag_recv.at[n], to, z)
        for n, to in enumerate((core, across, corner))
    ]
    for copy in flag_copies:
        copy.start()
    for k in range(CHUNKS):
        bas_copy(b, k, y_send, y_recv, across, True).start()
        bas_copy(b, k, core_send, core_recv, core, True).start()

    @pl.when(z == 0)
    def _():
        for k in range(CHUNKS):
            flow(2, k, True).start()

    for copy in own_copies[1:]:
        copy.wait()
    virt_up.wait_recv()
    virt_down.wait_recv()
    for w in range(3):
        turned = virt_band[w].astype(jnp.float32).T.astype(jnp.bfloat16)
        cols = pl.ds(w * width, width)
        virt_ext[pl.ds(width, blocks * width), cols] = turned
        virt_ext[pl.ds(0, width), cols] = turned[(blocks - 1) * width :]
        virt_ext[pl.ds((blocks + 1) * width, width), cols] = turned[:width]
    for n, sender in enumerate((core, across, corner)):
        remote(
            flag_rows.at[b], flag_rows.at[sender], flag_send.at[n], flag_recv.at[n], core, z
        ).wait_recv()
    flag_row = flag_rows[b, :1]
    part[z] = jnp.zeros((aux_rows, 128), jnp.float32)

    chi_lane = lax.broadcasted_iota(jnp.int32, (aux_rows, 128), 1)

    def two_columns(three, middle, t, acc):
        count = three.shape[1]
        row = lax.broadcasted_iota(jnp.int32, (count, 2 * count), 0)
        col = lax.broadcasted_iota(jnp.int32, (count, 2 * count), 1)
        same = jnp.where((col == row) | (col == row + count), 1.0, 0.0).astype(jnp.float32)
        left = lax.broadcasted_iota(jnp.int32, (aux_rows, 2 * count), 1) < count
        rows = three[...].reshape(aux_rows * count, band)
        ours = middle[pl.ds(2 * t, 2)].reshape(2 * count, band)
        prod = lax.dot_general(
            rows, ours, (((1,), (1,)), ((), ())), preferred_element_type=jnp.float32
        )
        kept = jnp.sum(prod.reshape(aux_rows, count, 2 * count) * same[None], axis=1)
        first = jnp.sum(jnp.where(left, kept, 0.0), axis=1, keepdims=True)
        second = jnp.sum(jnp.where(left, 0.0, kept), axis=1, keepdims=True)
        return jnp.where(chi_lane == 2 * t, first, jnp.where(chi_lane == 2 * t + 1, second, acc))

    nothing = jnp.zeros((aux_rows, 128), jnp.float32)

    def pair(three, middle):
        return lax.fori_loop(
            0, aux_rows // 2, lambda t, acc: two_columns(three, middle, t, acc), nothing
        )

    def middle_of(k):
        bas_copy(core, k, core_send, core_recv, core).wait_recv()
        bas_copy(corner, k, fwd_send, fwd_recv, core).wait_recv()

        def one_block(l, carry):
            rows = pl.ds(pl.multiple_of(l * width, width), width)
            virt = virt_ext[pl.ds(pl.multiple_of(l * width, width), band), :]
            three = ball[l, pl.ds(k * step, step)].reshape(step * width, band)
            three = three * flag_rows[l, :1].astype(jnp.bfloat16)
            value = jnp.dot(three, virt, preferred_element_type=jnp.float32)
            half[:, rows, :] = value.astype(jnp.bfloat16).reshape(step, width, band)
            return carry

        lax.fori_loop(0, blocks, one_block, 0)
        for q in range(step):
            value = jnp.dot(occ_ref[...], half[q], preferred_element_type=jnp.float32)
            mid[k * step + q] = (value * flag_row).astype(jnp.bfloat16)
        for at, f in ((2, 4), (3, 5)):
            @pl.when(z == at)
            def _():
                flow(f, k, True).start()

    def own_columns(k):
        for t in range(k * step // 2, (k + 1) * step // 2):
            part[z] = two_columns(ball.at[b], mid, t, part[z])

    for k in range(CHUNKS):
        bas_copy(across, k, y_send, y_recv, across).wait_recv()
        bas_copy(across, k, fwd_send, fwd_recv, core).start()
        relay(1, 0, k)
        relay(2, 1, k)
        if k >= 2:
            relay(2, 0, k - 2)
        if k:
            middle_of(k - 1)
        if k >= 2:
            relay(2, 5, k - 2)
            relay(1, 4, k - 2)
        if k >= 3:
            relay(1, 5, k - 3)
        if k:
            own_columns(k - 1)
    middle_of(CHUNKS - 1)
    relay(2, 0, 2)
    relay(2, 5, 2)
    own_columns(CHUNKS - 1)

    def chi_copy(other, turned, slot):
        src = part_t.at[other] if turned else part.at[other]
        to = (z, other) if turned == bool(slot) else (other, z)
        return remote(
            src, chi_in.at[b, slot], chi_send.at[other, int(turned)], chi_recv.at[b, slot], *to
        )

    def share(other, slot, acc):
        part[other] = acc
        full = jnp.concatenate([acc, jnp.zeros((128 - aux_rows, 128), jnp.float32)], 0)
        part_t[other] = full.T[:aux_rows]
        near = slot == 0
        chi_copy(other, not near, slot).start()

        @pl.when(b == other)
        def _():
            chi_in[b, slot] = part_t[other] if near else part[other]

        @pl.when(b != other)
        def _():
            chi_copy(other, near, slot).start()

    own = remote(part.at[z], chi_in.at[b, 0], chi_send.at[z, 0], chi_recv.at[b, 0], z, z)

    @pl.when(b == z)
    def _():
        chi_in[b, 0] = part[z]

    @pl.when(b != z)
    def _():
        own.start()

    relay(2, 0, 3)

    @pl.when(z == 1)
    def _():
        arrived(2)
        share(0, 0, pair(zall.at[0], mid))

    @pl.when(z == 2)
    def _():
        arrived(3)
        share(3, 0, pair(zall.at[3], mid))

    relay(2, 5, 3)

    @pl.when(z >= 2)
    def _():
        for i in (1, 0):
            @pl.when(z == 3)
            def _():
                arrived(i)
            share(i, 0, pair(zall.at[i, :, pl.ds(0, early)], mid.at[:, pl.ds(0, early)]))

    @pl.when(z <= 1)
    def _():
        acc = {2: nothing, 3: nothing}
        for i, k in ((2, 0), (2, 1), (3, 0), (2, 2), (3, 1), (2, 3), (3, 2), (3, 3)):
            @pl.when(z == 0)
            def _():
                flow(i + 2, k, False).wait_recv()
            if (i, k) not in ((2, 0), (2, 1), (3, 0)):
                relay(1, i + 2, k)
            for t in range(k * step // 2, (k + 1) * step // 2):
                acc[i] = two_columns(ball.at[b, :, pl.ds(early, late)], mall.at[i - 2], t, acc[i])
            if k == CHUNKS - 1:
                share(i, 1, acc[i])

    top = jnp.maximum(b, z)
    low = jnp.minimum(b, z)
    owner = jnp.where((top == 3) & (low == 2), 2, top)
    split = (low <= 1) & (top >= 2)

    def chi_arrived(k, slot):
        remote(
            part.at[0], chi_in.at[k, slot], chi_send.at[0, 0], chi_recv.at[k, slot], b, z_right
        ).wait_recv()

    for k in range(blocks):
        @pl.when((b != k) | (owner != z))
        def _():
            chi_arrived(k, 0)

        @pl.when(split & ((b != k) | (low != z)))
        def _():
            chi_arrived(k, 1)
    total = chi_in[0, 0] + chi_in[1, 0] + chi_in[2, 0] + chi_in[3, 0]
    out_ref[...] = total[:, : out_ref.shape[1]] * scale

    @pl.when(split)
    def _():
        rest = chi_in[0, 1] + chi_in[1, 1] + chi_in[2, 1] + chi_in[3, 1]
        out_ref[...] = (total + rest)[:, : out_ref.shape[1]] * scale

    virt_up.wait_send()
    virt_down.wait_send()
    for copy in flag_copies:
        copy.wait_send()
    for k in range(CHUNKS):
        bas_copy(b, k, y_send, y_recv, across, True).wait_send()
        bas_copy(b, k, core_send, core_recv, core, True).wait_send()
        bas_copy(across, k, fwd_send, fwd_recv, core).wait_send()
    for at, f, first in (
        (0, 0, True), (1, 0, False), (2, 0, False), (1, 1, True), (2, 1, False), (0, 2, True),
        (3, 3, True), (2, 4, True), (1, 4, False), (3, 5, True), (2, 5, False), (1, 5, False),
    ):
        @pl.when(z == at)
        def _():
            for k in range(CHUNKS):
                flow(f, k, first).wait_send()

    @pl.when(b != z)
    def _():
        own.wait_send()

    def shared(other, slot):
        near = slot == 0
        chi_copy(other, not near, slot).wait_send()

        @pl.when(b != other)
        def _():
            chi_copy(other, near, slot).wait_send()

    for at, other, slot in (
        (0, 2, 1), (0, 3, 1), (1, 0, 0), (1, 2, 1), (1, 3, 1),
        (2, 0, 0), (2, 1, 0), (2, 3, 0), (3, 0, 0), (3, 1, 0),
    ):
        @pl.when(z == at)
        def _():
            shared(other, slot)


def one_kernel(three_index, screen, green_occ, green_virt):
    aux_rows, width, band = three_index.shape
    nbasis = green_virt.shape[1]
    scale = -2.0 / math.sqrt(3 * width * width)
    bf16, f32 = jnp.bfloat16, jnp.float32
    dma = pltpu.SemaphoreType.DMA
    return pl.pallas_call(
        functools.partial(kernel, scale),
        out_shape=jax.ShapeDtypeStruct((aux_rows, aux_rows), f32),
        in_specs=[pl.BlockSpec(memory_space=pl.ANY)] * 4,
        out_specs=pl.BlockSpec(memory_space=pltpu.VMEM),
        scratch_shapes=[
            pltpu.VMEM((4, aux_rows, width, band), bf16),
            pltpu.VMEM((4, aux_rows, width, band), bf16),
            pltpu.VMEM((2, aux_rows, 3 * width // 8, band), bf16),
            pltpu.VMEM((aux_rows, width, band), bf16),
            pltpu.VMEM((aux_rows // CHUNKS, nbasis, band), bf16),
            pltpu.VMEM((width, nbasis), bf16),
            pltpu.VMEM((3, width, nbasis), bf16),
            pltpu.VMEM((nbasis + 2 * width, band), bf16),
            pltpu.SMEM((1, 3), jnp.int32),
            pltpu.VMEM((4, 8, band), f32),
            pltpu.VMEM((4, aux_rows, 128), f32),
            pltpu.VMEM((4, aux_rows, 128), f32),
            pltpu.VMEM((4, 2, aux_rows, 128), f32),
        ]
        + [dma((CHUNKS,))] * 6
        + [dma((2,))] * 2
        + [dma((6, CHUNKS))] * 2
        + [dma((4, 2)), dma((4, 2)), dma((3,)), dma((3,)), dma((4,))],
        compiler_params=pltpu.CompilerParams(
            collective_id=0, has_side_effects=True, vmem_limit_bytes=56 * 1024 * 1024
        ),
    )(three_index, screen, green_occ, green_virt)


def padded_2(x, sides, width):
    for axis, dim in sides:
        count, length = (lax.axis_size(axis), x.shape[dim])
        up = [(i, (i + 1) % count) for i in range(count)]
        down = [(j, i) for i, j in up]
        last = lax.slice_in_dim(x, length - width, length, axis=dim)
        initial = lax.slice_in_dim(x, 0, width, axis=dim)
        before = lax.ppermute(last, axis, up)
        after = lax.ppermute(initial, axis, down)
        x = jnp.concatenate([before, x, after], axis=dim)
    return x


def body(three_index, screen, green_occ, green_virt):
    width = green_virt.shape[0]
    aux_rows = three_index.shape[0]
    nbasis = green_virt.shape[1]
    screen_flags = screen[0].astype(jnp.bfloat16)
    masked = (
        three_index.reshape(aux_rows, width, 3, width) * screen_flags[None, None, :, None]
    ).reshape(aux_rows, width, 3 * width)
    virt_rows = padded_2(green_virt, (("bas", 0),), width)
    half = jnp.dot(
        masked.reshape(aux_rows * width, 3 * width), virt_rows, preferred_element_type=jnp.float32
    )
    half = half.astype(jnp.bfloat16).reshape(aux_rows, width, nbasis)
    padded = jnp.concatenate([half[:, :, nbasis - width :], half, half[:, :, :width]], 2)

    def one_block(offset):
        begin = offset * width
        occ_cols = lax.dynamic_slice_in_dim(green_occ, begin, width, 1)
        virt_band = lax.dynamic_slice_in_dim(padded, begin, 3 * width, 2)
        return jnp.einsum("lm,alc->mac", occ_cols, virt_band, preferred_element_type=jnp.float32)

    parts_out = lax.map(
        one_block, jnp.arange(lax.axis_size("bas") * width // width, dtype=jnp.int32)
    )
    summed = lax.psum_scatter(
        parts_out.reshape(lax.axis_size("bas") * width, aux_rows, 3 * width),
        "bas",
        scatter_dimension=0,
        tiled=True,
    )
    middle = jnp.transpose(summed, (1, 0, 2)).astype(jnp.bfloat16)
    partial_chi = jnp.einsum(
        "pmc,qmc->pq",
        masked,
        lax.all_gather(middle, "aux", axis=0, tiled=True),
        preferred_element_type=jnp.float32,
    )
    summed_chi = lax.psum_scatter(partial_chi, "bas", scatter_dimension=1, tiled=True)
    return summed_chi * (-2.0 / math.sqrt(3 * width * width))


def solution(mesh):
    in_specs = (
        P(("grp", "aux"), "bas", None),
        P(("grp", "bas"), None),
        P(("grp", "bas"), None),
        P(("grp", "bas"), None),
    )
    out_specs = P(("grp", "aux"), "bas")
    fits = mesh.shape["bas"] == 4 and mesh.shape["aux"] == 4
    return jax.shard_map(one_kernel if fits else body, mesh=mesh, in_specs=in_specs, out_specs=out_specs, check_vma=False)
```

```python
import functools
import math

import jax
import jax.numpy as jnp
from jax import lax
from jax.experimental import pallas as pl
from jax.experimental.pallas import tpu as pltpu
from jax.sharding import PartitionSpec as P

MESH = pl.DeviceIdType.MESH
CHUNKS = 4


def kernel(
    scale,
    three_ref, screen_ref, occ_hbm, virt_hbm, out_ref,
    ball, zall, mall, mid, half, occ_ref, virt_band, virt_ext, flags_ref, flag_rows, part, part_t, chi_in,
    y_send, y_recv, core_send, core_recv, fwd_send, fwd_recv,
    virt_send, virt_recv, z_send, z_recv, chi_send, chi_recv, flag_send, flag_recv, local_sem,
):
    aux_rows, width, band = three_ref.shape
    blocks = 4
    step = aux_rows // CHUNKS
    late = 3 * width // 8
    early = width - late
    g, b, z = lax.axis_index("grp"), lax.axis_index("bas"), lax.axis_index("aux")
    core = b + 1 - 2 * lax.rem(b, 2)
    across = lax.rem(b + 2, blocks)
    corner = blocks - 1 - b
    above, below = lax.rem(b + 1, blocks), lax.rem(b + blocks - 1, blocks)

    barrier = pltpu.get_barrier_semaphore()
    for k in range(1, 16):
        other = lax.rem(b * 4 + z + k, 16)
        pl.semaphore_signal(
            barrier, inc=1, device_id=(g, other // 4, lax.rem(other, 4)), device_id_type=MESH
        )

    own_copies = [
        pltpu.make_async_copy(screen_ref, flags_ref, local_sem.at[0]),
        pltpu.make_async_copy(three_ref, ball.at[b], local_sem.at[1]),
        pltpu.make_async_copy(virt_hbm, virt_band.at[1], local_sem.at[2]),
        pltpu.make_async_copy(occ_hbm, occ_ref, local_sem.at[3]),
    ]
    for copy in own_copies:
        copy.start()
    own_copies[0].wait()
    lane = lax.broadcasted_iota(jnp.int32, (8, band), 1)
    flags = [flags_ref[0, w].astype(jnp.float32) for w in range(3)]
    flag_rows[b] = jnp.where(lane < width, flags[0], jnp.where(lane < 2 * width, flags[1], flags[2]))
    pl.semaphore_wait(barrier, 15)

    def remote(src, dst, send, recv, bas, aux):
        return pltpu.make_async_remote_copy(
            src_ref=src, dst_ref=dst, send_sem=send, recv_sem=recv,
            device_id=(g, bas, aux), device_id_type=MESH,
        )

    def bas_copy(block, k, sends, recvs, to, first=False):
        rows = ball.at[block, pl.ds(k * step, step)]
        src = three_ref.at[pl.ds(k * step, step)] if first else rows
        return remote(src, rows, sends.at[k], recvs.at[k], to, z)

    z_right, z_left = lax.rem(z + 1, 4), lax.rem(z + 3, 4)

    def flow(f, k, first):
        aux = pl.ds(k * step, step)
        if f >= 4:
            dst = mall.at[f - 4, aux]
            src = mid.at[aux, pl.ds(early, late)] if first else dst
        else:
            rows = (pl.ds(0, early), pl.ds(0, early), pl.ds(early, late), pl.ds(0, width))[f]
            dst = zall.at[(0, 1, 0, 3)[f], aux, rows]
            src = three_ref.at[aux, rows] if first else dst
        to = z_right if f < 3 else lax.rem(z + 2, 4) if f == 5 and first else z_left
        return remote(src, dst, z_send.at[f, k], z_recv.at[f, k], b, to)

    def relay(at, f, k):
        @pl.when(z == at)
        def _():
            flow(f, k, False).wait_recv()
            flow(f, k, False).start()

    def arrived(f):
        for k in range(CHUNKS):
            flow(f, k, False).wait_recv()

    virt_up = remote(virt_hbm, virt_band.at[0], virt_send.at[0], virt_recv.at[0], above, z)
    virt_down = remote(virt_hbm, virt_band.at[2], virt_send.at[1], virt_recv.at[1], below, z)
    for at, f in ((0, 0), (1, 1), (3, 3)):
        @pl.when(z == at)
        def _():
            for k in range(CHUNKS):
                flow(f, k, True).start()
    virt_up.start()
    virt_down.start()
    flag_copies = [
        remote(flag_rows.at[b], flag_rows.at[b], flag_send.at[n], flag_recv.at[n], to, z)
        for n, to in enumerate((core, across, corner))
    ]
    for copy in flag_copies:
        copy.start()
    for k in range(CHUNKS):
        bas_copy(b, k, y_send, y_recv, across, True).start()
        bas_copy(b, k, core_send, core_recv, core, True).start()

    @pl.when(z == 0)
    def _():
        for k in range(CHUNKS):
            flow(2, k, True).start()

    for copy in own_copies[1:]:
        copy.wait()
    virt_up.wait_recv()
    virt_down.wait_recv()
    for w in range(3):
        turned = virt_band[w].astype(jnp.float32).T.astype(jnp.bfloat16)
        cols = pl.ds(w * width, width)
        virt_ext[pl.ds(width, blocks * width), cols] = turned
        virt_ext[pl.ds(0, width), cols] = turned[(blocks - 1) * width :]
        virt_ext[pl.ds((blocks + 1) * width, width), cols] = turned[:width]
    for n, sender in enumerate((core, across, corner)):
        remote(
            flag_rows.at[b], flag_rows.at[sender], flag_send.at[n], flag_recv.at[n], core, z
        ).wait_recv()
    flag_row = flag_rows[b, :1]
    part[z] = jnp.zeros((aux_rows, 128), jnp.float32)

    chi_lane = lax.broadcasted_iota(jnp.int32, (aux_rows, 128), 1)

    def two_columns(three, middle, t, acc):
        count = three.shape[1]
        row = lax.broadcasted_iota(jnp.int32, (count, 2 * count), 0)
        col = lax.broadcasted_iota(jnp.int32, (count, 2 * count), 1)
        same = jnp.where((col == row) | (col == row + count), 1.0, 0.0).astype(jnp.float32)
        left = lax.broadcasted_iota(jnp.int32, (aux_rows, 2 * count), 1) < count
        rows = three[...].reshape(aux_rows * count, band)
        ours = middle[pl.ds(2 * t, 2)].reshape(2 * count, band)
        prod = lax.dot_general(
            rows, ours, (((1,), (1,)), ((), ())), preferred_element_type=jnp.float32
        )
        kept = jnp.sum(prod.reshape(aux_rows, count, 2 * count) * same[None], axis=1)
        first = jnp.sum(jnp.where(left, kept, 0.0), axis=1, keepdims=True)
        second = jnp.sum(jnp.where(left, 0.0, kept), axis=1, keepdims=True)
        return jnp.where(chi_lane == 2 * t, first, jnp.where(chi_lane == 2 * t + 1, second, acc))

    nothing = jnp.zeros((aux_rows, 128), jnp.float32)

    def pair(three, middle):
        return lax.fori_loop(
            0, aux_rows // 2, lambda t, acc: two_columns(three, middle, t, acc), nothing
        )

    def middle_of(k):
        bas_copy(core, k, core_send, core_recv, core).wait_recv()
        bas_copy(corner, k, fwd_send, fwd_recv, core).wait_recv()

        def one_block(l, carry):
            rows = pl.ds(pl.multiple_of(l * width, width), width)
            virt = virt_ext[pl.ds(pl.multiple_of(l * width, width), band), :]
            three = ball[l, pl.ds(k * step, step)].reshape(step * width, band)
            three = three * flag_rows[l, :1].astype(jnp.bfloat16)
            value = jnp.dot(three, virt, preferred_element_type=jnp.float32)
            half[:, rows, :] = value.astype(jnp.bfloat16).reshape(step, width, band)
            return carry

        lax.fori_loop(0, blocks, one_block, 0)
        for q in range(step):
            value = jnp.dot(occ_ref[...], half[q], preferred_element_type=jnp.float32)
            mid[k * step + q] = (value * flag_row).astype(jnp.bfloat16)
        for at, f in ((2, 4), (3, 5)):
            @pl.when(z == at)
            def _():
                flow(f, k, True).start()

    def own_columns(k):
        for t in range(k * step // 2, (k + 1) * step // 2):
            part[z] = two_columns(ball.at[b], mid, t, part[z])

    upward = {
        1: [(0, k) for k in range(CHUNKS)] + [None] * CHUNKS,
        2: [(1, k) for k in range(CHUNKS)] + [(0, k) for k in range(CHUNKS)],
    }

    def pass_up(n):
        for at, chunks in upward.items():
            if chunks[n] is not None:
                relay(at, *chunks[n])

    for k in range(CHUNKS):
        pass_up(2 * k)
        bas_copy(across, k, y_send, y_recv, across).wait_recv()
        bas_copy(across, k, fwd_send, fwd_recv, core).start()
        pass_up(2 * k + 1)
        if k:
            middle_of(k - 1)
        if k >= 2:
            relay(1, 4, k - 2)
            relay(1, 5, k - 2)
        if k:
            own_columns(k - 1)
    middle_of(CHUNKS - 1)
    own_columns(CHUNKS - 1)

    def chi_copy(other, turned, slot):
        src = part_t.at[other] if turned else part.at[other]
        to = (z, other) if turned == bool(slot) else (other, z)
        return remote(
            src, chi_in.at[b, slot], chi_send.at[other, int(turned)], chi_recv.at[b, slot], *to
        )

    def share(other, slot, acc):
        part[other] = acc
        full = jnp.concatenate([acc, jnp.zeros((128 - aux_rows, 128), jnp.float32)], 0)
        part_t[other] = full.T[:aux_rows]
        near = slot == 0
        chi_copy(other, not near, slot).start()

        @pl.when(b == other)
        def _():
            chi_in[b, slot] = part_t[other] if near else part[other]

        @pl.when(b != other)
        def _():
            chi_copy(other, near, slot).start()

    own = remote(part.at[z], chi_in.at[b, 0], chi_send.at[z, 0], chi_recv.at[b, 0], z, z)

    @pl.when(b == z)
    def _():
        chi_in[b, 0] = part[z]

    @pl.when(b != z)
    def _():
        own.start()

    @pl.when(z == 1)
    def _():
        arrived(2)
        share(0, 0, pair(zall.at[0], mid))

    @pl.when(z == 2)
    def _():
        arrived(3)
        share(3, 0, pair(zall.at[3], mid))

    @pl.when(z >= 2)
    def _():
        for i in (1, 0):
            @pl.when(z == 3)
            def _():
                arrived(i)
            share(i, 0, pair(zall.at[i, :, pl.ds(0, early)], mid.at[:, pl.ds(0, early)]))

    @pl.when(z <= 1)
    def _():
        acc = {2: nothing, 3: nothing}
        for i, k in ((2, 0), (3, 0), (2, 1), (3, 1), (2, 2), (3, 2), (2, 3), (3, 3)):
            @pl.when(z == 0)
            def _():
                flow(i + 2, k, False).wait_recv()
            if k >= 2:
                relay(1, i + 2, k)
            for t in range(k * step // 2, (k + 1) * step // 2):
                acc[i] = two_columns(ball.at[b, :, pl.ds(early, late)], mall.at[i - 2], t, acc[i])
            if k == CHUNKS - 1:
                share(i, 1, acc[i])

    top = jnp.maximum(b, z)
    low = jnp.minimum(b, z)
    owner = jnp.where((top == 3) & (low == 2), 2, top)
    split = (low <= 1) & (top >= 2)

    def chi_arrived(k, slot):
        remote(
            part.at[0], chi_in.at[k, slot], chi_send.at[0, 0], chi_recv.at[k, slot], b, z_right
        ).wait_recv()

    for k in range(blocks):
        @pl.when((b != k) | (owner != z))
        def _():
            chi_arrived(k, 0)

        @pl.when(split & ((b != k) | (low != z)))
        def _():
            chi_arrived(k, 1)
    total = chi_in[0, 0] + chi_in[1, 0] + chi_in[2, 0] + chi_in[3, 0]
    out_ref[...] = total[:, : out_ref.shape[1]] * scale

    @pl.when(split)
    def _():
        rest = chi_in[0, 1] + chi_in[1, 1] + chi_in[2, 1] + chi_in[3, 1]
        out_ref[...] = (total + rest)[:, : out_ref.shape[1]] * scale

    virt_up.wait_send()
    virt_down.wait_send()
    for copy in flag_copies:
        copy.wait_send()
    for k in range(CHUNKS):
        bas_copy(b, k, y_send, y_recv, across, True).wait_send()
        bas_copy(b, k, core_send, core_recv, core, True).wait_send()
        bas_copy(across, k, fwd_send, fwd_recv, core).wait_send()
    for at, f, first in (
        (0, 0, True), (1, 0, False), (2, 0, False), (1, 1, True), (2, 1, False), (0, 2, True),
        (3, 3, True), (2, 4, True), (1, 4, False), (3, 5, True), (1, 5, False),
    ):
        @pl.when(z == at)
        def _():
            for k in range(CHUNKS):
                flow(f, k, first).wait_send()

    @pl.when(b != z)
    def _():
        own.wait_send()

    def shared(other, slot):
        near = slot == 0
        chi_copy(other, not near, slot).wait_send()

        @pl.when(b != other)
        def _():
            chi_copy(other, near, slot).wait_send()

    for at, other, slot in (
        (0, 2, 1), (0, 3, 1), (1, 0, 0), (1, 2, 1), (1, 3, 1),
        (2, 0, 0), (2, 1, 0), (2, 3, 0), (3, 0, 0), (3, 1, 0),
    ):
        @pl.when(z == at)
        def _():
            shared(other, slot)


def one_kernel(three_index, screen, green_occ, green_virt):
    aux_rows, width, band = three_index.shape
    nbasis = green_virt.shape[1]
    scale = -2.0 / math.sqrt(3 * width * width)
    bf16, f32 = jnp.bfloat16, jnp.float32
    dma = pltpu.SemaphoreType.DMA
    return pl.pallas_call(
        functools.partial(kernel, scale),
        out_shape=jax.ShapeDtypeStruct((aux_rows, aux_rows), f32),
        in_specs=[pl.BlockSpec(memory_space=pl.ANY)] * 4,
        out_specs=pl.BlockSpec(memory_space=pltpu.VMEM),
        scratch_shapes=[
            pltpu.VMEM((4, aux_rows, width, band), bf16),
            pltpu.VMEM((4, aux_rows, width, band), bf16),
            pltpu.VMEM((2, aux_rows, 3 * width // 8, band), bf16),
            pltpu.VMEM((aux_rows, width, band), bf16),
            pltpu.VMEM((aux_rows // CHUNKS, nbasis, band), bf16),
            pltpu.VMEM((width, nbasis), bf16),
            pltpu.VMEM((3, width, nbasis), bf16),
            pltpu.VMEM((nbasis + 2 * width, band), bf16),
            pltpu.SMEM((1, 3), jnp.int32),
            pltpu.VMEM((4, 8, band), f32),
            pltpu.VMEM((4, aux_rows, 128), f32),
            pltpu.VMEM((4, aux_rows, 128), f32),
            pltpu.VMEM((4, 2, aux_rows, 128), f32),
        ]
        + [dma((CHUNKS,))] * 6
        + [dma((2,))] * 2
        + [dma((6, CHUNKS))] * 2
        + [dma((4, 2)), dma((4, 2)), dma((3,)), dma((3,)), dma((4,))],
        compiler_params=pltpu.CompilerParams(
            collective_id=0, has_side_effects=True, vmem_limit_bytes=56 * 1024 * 1024
        ),
    )(three_index, screen, green_occ, green_virt)


def padded_2(x, sides, width):
    for axis, dim in sides:
        count, length = (lax.axis_size(axis), x.shape[dim])
        up = [(i, (i + 1) % count) for i in range(count)]
        down = [(j, i) for i, j in up]
        last = lax.slice_in_dim(x, length - width, length, axis=dim)
        initial = lax.slice_in_dim(x, 0, width, axis=dim)
        before = lax.ppermute(last, axis, up)
        after = lax.ppermute(initial, axis, down)
        x = jnp.concatenate([before, x, after], axis=dim)
    return x


def body(three_index, screen, green_occ, green_virt):
    width = green_virt.shape[0]
    aux_rows = three_index.shape[0]
    nbasis = green_virt.shape[1]
    screen_flags = screen[0].astype(jnp.bfloat16)
    masked = (
        three_index.reshape(aux_rows, width, 3, width) * screen_flags[None, None, :, None]
    ).reshape(aux_rows, width, 3 * width)
    virt_rows = padded_2(green_virt, (("bas", 0),), width)
    half = jnp.dot(
        masked.reshape(aux_rows * width, 3 * width), virt_rows, preferred_element_type=jnp.float32
    )
    half = half.astype(jnp.bfloat16).reshape(aux_rows, width, nbasis)
    padded = jnp.concatenate([half[:, :, nbasis - width :], half, half[:, :, :width]], 2)

    def one_block(offset):
        begin = offset * width
        occ_cols = lax.dynamic_slice_in_dim(green_occ, begin, width, 1)
        virt_band = lax.dynamic_slice_in_dim(padded, begin, 3 * width, 2)
        return jnp.einsum("lm,alc->mac", occ_cols, virt_band, preferred_element_type=jnp.float32)

    parts_out = lax.map(
        one_block, jnp.arange(lax.axis_size("bas") * width // width, dtype=jnp.int32)
    )
    summed = lax.psum_scatter(
        parts_out.reshape(lax.axis_size("bas") * width, aux_rows, 3 * width),
        "bas",
        scatter_dimension=0,
        tiled=True,
    )
    middle = jnp.transpose(summed, (1, 0, 2)).astype(jnp.bfloat16)
    partial_chi = jnp.einsum(
        "pmc,qmc->pq",
        masked,
        lax.all_gather(middle, "aux", axis=0, tiled=True),
        preferred_element_type=jnp.float32,
    )
    summed_chi = lax.psum_scatter(partial_chi, "bas", scatter_dimension=1, tiled=True)
    return summed_chi * (-2.0 / math.sqrt(3 * width * width))


def solution(mesh):
    in_specs = (
        P(("grp", "aux"), "bas", None),
        P(("grp", "bas"), None),
        P(("grp", "bas"), None),
        P(("grp", "bas"), None),
    )
    out_specs = P(("grp", "aux"), "bas")
    fits = mesh.shape["bas"] == 4 and mesh.shape["aux"] == 4
    return jax.shard_map(one_kernel if fits else body, mesh=mesh, in_specs=in_specs, out_specs=out_specs, check_vma=False)
```

```python
import functools
import math

import jax
import jax.numpy as jnp
from jax import lax
from jax.experimental import pallas as pl
from jax.experimental.pallas import tpu as pltpu
from jax.sharding import PartitionSpec as P

MESH = pl.DeviceIdType.MESH
CHUNKS = 4


def kernel(
    scale,
    three_ref, screen_ref, occ_hbm, virt_hbm, out_ref,
    ball, zall, mall, mid, half, occ_ref, virt_band, virt_ext, flags_ref, flag_rows, part, part_t, chi_in,
    y_send, y_recv, core_send, core_recv, fwd_send, fwd_recv,
    virt_send, virt_recv, z_send, z_recv, chi_send, chi_recv, flag_send, flag_recv, local_sem,
):
    aux_rows, width, band = three_ref.shape
    blocks = 4
    step = aux_rows // CHUNKS
    late = 3 * width // 8
    early = width - late
    g, b, z = lax.axis_index("grp"), lax.axis_index("bas"), lax.axis_index("aux")
    core = b + 1 - 2 * lax.rem(b, 2)
    across = lax.rem(b + 2, blocks)
    corner = blocks - 1 - b
    above, below = lax.rem(b + 1, blocks), lax.rem(b + blocks - 1, blocks)

    barrier = pltpu.get_barrier_semaphore()
    for k in range(1, 16):
        other = lax.rem(b * 4 + z + k, 16)
        pl.semaphore_signal(
            barrier, inc=1, device_id=(g, other // 4, lax.rem(other, 4)), device_id_type=MESH
        )

    own_copies = [
        pltpu.make_async_copy(screen_ref, flags_ref, local_sem.at[0]),
        pltpu.make_async_copy(three_ref, ball.at[b], local_sem.at[1]),
        pltpu.make_async_copy(virt_hbm, virt_band.at[1], local_sem.at[2]),
        pltpu.make_async_copy(occ_hbm, occ_ref, local_sem.at[3]),
    ]
    for copy in own_copies:
        copy.start()
    own_copies[0].wait()
    lane = lax.broadcasted_iota(jnp.int32, (8, band), 1)
    flags = [flags_ref[0, w].astype(jnp.float32) for w in range(3)]
    flag_rows[b] = jnp.where(lane < width, flags[0], jnp.where(lane < 2 * width, flags[1], flags[2]))
    pl.semaphore_wait(barrier, 15)

    def remote(src, dst, send, recv, bas, aux):
        return pltpu.make_async_remote_copy(
            src_ref=src, dst_ref=dst, send_sem=send, recv_sem=recv,
            device_id=(g, bas, aux), device_id_type=MESH,
        )

    def bas_copy(block, k, sends, recvs, to, first=False):
        rows = ball.at[block, pl.ds(k * step, step)]
        src = three_ref.at[pl.ds(k * step, step)] if first else rows
        return remote(src, rows, sends.at[k], recvs.at[k], to, z)

    z_right, z_left = lax.rem(z + 1, 4), lax.rem(z + 3, 4)

    def flow(f, k, first):
        aux = pl.ds(k * step, step)
        if f >= 4:
            dst = mall.at[f - 4, aux]
            src = mid.at[aux, pl.ds(early, late)] if first else dst
        else:
            rows = (pl.ds(0, early), pl.ds(0, early), pl.ds(early, late), pl.ds(0, width))[f]
            dst = zall.at[(0, 1, 0, 3)[f], aux, rows]
            src = three_ref.at[aux, rows] if first else dst
        to = z_right if f < 3 else lax.rem(z + 2, 4) if f == 5 and first else z_left
        return remote(src, dst, z_send.at[f, k], z_recv.at[f, k], b, to)

    def relay(at, f, k):
        @pl.when(z == at)
        def _():
            flow(f, k, False).wait_recv()
            flow(f, k, False).start()

    def arrived(f):
        for k in range(CHUNKS):
            flow(f, k, False).wait_recv()

    virt_up = remote(virt_hbm, virt_band.at[0], virt_send.at[0], virt_recv.at[0], above, z)
    virt_down = remote(virt_hbm, virt_band.at[2], virt_send.at[1], virt_recv.at[1], below, z)
    for at, f in ((0, 0), (1, 1), (3, 3)):
        @pl.when(z == at)
        def _():
            for k in range(CHUNKS):
                flow(f, k, True).start()
    virt_up.start()
    virt_down.start()
    flag_copies = [
        remote(flag_rows.at[b], flag_rows.at[b], flag_send.at[n], flag_recv.at[n], to, z)
        for n, to in enumerate((core, across, corner))
    ]
    for copy in flag_copies:
        copy.start()
    for k in range(CHUNKS):
        bas_copy(b, k, y_send, y_recv, across, True).start()
        bas_copy(b, k, core_send, core_recv, core, True).start()

    @pl.when(z == 0)
    def _():
        for k in range(CHUNKS):
            flow(2, k, True).start()

    for copy in own_copies[1:]:
        copy.wait()
    virt_up.wait_recv()
    virt_down.wait_recv()
    for w in range(3):
        turned = virt_band[w].astype(jnp.float32).T.astype(jnp.bfloat16)
        cols = pl.ds(w * width, width)
        virt_ext[pl.ds(width, blocks * width), cols] = turned
        virt_ext[pl.ds(0, width), cols] = turned[(blocks - 1) * width :]
        virt_ext[pl.ds((blocks + 1) * width, width), cols] = turned[:width]
    for n, sender in enumerate((core, across, corner)):
        remote(
            flag_rows.at[b], flag_rows.at[sender], flag_send.at[n], flag_recv.at[n], core, z
        ).wait_recv()
    flag_row = flag_rows[b, :1]
    part[z] = jnp.zeros((aux_rows, 128), jnp.float32)

    chi_lane = lax.broadcasted_iota(jnp.int32, (aux_rows, 128), 1)

    def two_columns(three, middle, t, acc):
        count = three.shape[1]
        row = lax.broadcasted_iota(jnp.int32, (count, 2 * count), 0)
        col = lax.broadcasted_iota(jnp.int32, (count, 2 * count), 1)
        same = jnp.where((col == row) | (col == row + count), 1.0, 0.0).astype(jnp.float32)
        left = lax.broadcasted_iota(jnp.int32, (aux_rows, 2 * count), 1) < count
        rows = three[...].reshape(aux_rows * count, band)
        ours = middle[pl.ds(2 * t, 2)].reshape(2 * count, band)
        prod = lax.dot_general(
            rows, ours, (((1,), (1,)), ((), ())), preferred_element_type=jnp.float32
        )
        kept = jnp.sum(prod.reshape(aux_rows, count, 2 * count) * same[None], axis=1)
        first = jnp.sum(jnp.where(left, kept, 0.0), axis=1, keepdims=True)
        second = jnp.sum(jnp.where(left, 0.0, kept), axis=1, keepdims=True)
        return jnp.where(chi_lane == 2 * t, first, jnp.where(chi_lane == 2 * t + 1, second, acc))

    nothing = jnp.zeros((aux_rows, 128), jnp.float32)

    def pair(three, middle):
        return lax.fori_loop(
            0, aux_rows // 2, lambda t, acc: two_columns(three, middle, t, acc), nothing
        )

    def middle_of(k):
        bas_copy(core, k, core_send, core_recv, core).wait_recv()
        bas_copy(corner, k, fwd_send, fwd_recv, core).wait_recv()

        def one_block(l, carry):
            rows = pl.ds(pl.multiple_of(l * width, width), width)
            virt = virt_ext[pl.ds(pl.multiple_of(l * width, width), band), :]
            three = ball[l, pl.ds(k * step, step)].reshape(step * width, band)
            three = three * flag_rows[l, :1].astype(jnp.bfloat16)
            value = jnp.dot(three, virt, preferred_element_type=jnp.float32)
            half[:, rows, :] = value.astype(jnp.bfloat16).reshape(step, width, band)
            return carry

        lax.fori_loop(0, blocks, one_block, 0)
        for q in range(step):
            value = jnp.dot(occ_ref[...], half[q], preferred_element_type=jnp.float32)
            mid[k * step + q] = (value * flag_row).astype(jnp.bfloat16)
        for at, f in ((2, 4), (3, 5)):
            @pl.when(z == at)
            def _():
                flow(f, k, True).start()

    def own_columns(k):
        for t in range(k * step // 2, (k + 1) * step // 2):
            part[z] = two_columns(ball.at[b], mid, t, part[z])

    upward = {
        1: [(0, k) for k in range(CHUNKS)] + [None] * CHUNKS,
        2: [(1, k) for k in range(CHUNKS)] + [(0, k) for k in range(CHUNKS)],
    }

    def pass_up(n):
        for at, chunks in upward.items():
            if chunks[n] is not None:
                relay(at, *chunks[n])

    for k in range(CHUNKS):
        pass_up(2 * k)
        bas_copy(across, k, y_send, y_recv, across).wait_recv()
        bas_copy(across, k, fwd_send, fwd_recv, core).start()
        pass_up(2 * k + 1)
        middle_of(k)
        if k:
            relay(1, 4, k - 1)
            relay(1, 5, k - 1)
        own_columns(k)

    def chi_copy(other, turned, slot):
        src = part_t.at[other] if turned else part.at[other]
        to = (z, other) if turned == bool(slot) else (other, z)
        return remote(
            src, chi_in.at[b, slot], chi_send.at[other, int(turned)], chi_recv.at[b, slot], *to
        )

    def share(other, slot, acc):
        part[other] = acc
        full = jnp.concatenate([acc, jnp.zeros((128 - aux_rows, 128), jnp.float32)], 0)
        part_t[other] = full.T[:aux_rows]
        near = slot == 0
        chi_copy(other, not near, slot).start()

        @pl.when(b == other)
        def _():
            chi_in[b, slot] = part_t[other] if near else part[other]

        @pl.when(b != other)
        def _():
            chi_copy(other, near, slot).start()

    own = remote(part.at[z], chi_in.at[b, 0], chi_send.at[z, 0], chi_recv.at[b, 0], z, z)

    @pl.when(b == z)
    def _():
        chi_in[b, 0] = part[z]

    @pl.when(b != z)
    def _():
        own.start()

    @pl.when(z == 1)
    def _():
        arrived(2)
        share(0, 0, pair(zall.at[0], mid))

    @pl.when(z == 2)
    def _():
        arrived(3)
        share(3, 0, pair(zall.at[3], mid))

    @pl.when(z >= 2)
    def _():
        for i in (1, 0):
            @pl.when(z == 3)
            def _():
                arrived(i)
            share(i, 0, pair(zall.at[i, :, pl.ds(0, early)], mid.at[:, pl.ds(0, early)]))

    @pl.when(z <= 1)
    def _():
        acc = {2: nothing, 3: nothing}
        for i, k in ((2, 0), (3, 0), (2, 1), (3, 1), (2, 2), (3, 2), (2, 3), (3, 3)):
            @pl.when(z == 0)
            def _():
                flow(i + 2, k, False).wait_recv()
            if k == CHUNKS - 1:
                relay(1, i + 2, k)
            for t in range(k * step // 2, (k + 1) * step // 2):
                acc[i] = two_columns(ball.at[b, :, pl.ds(early, late)], mall.at[i - 2], t, acc[i])
            if k == CHUNKS - 1:
                share(i, 1, acc[i])

    top = jnp.maximum(b, z)
    low = jnp.minimum(b, z)
    owner = jnp.where((top == 3) & (low == 2), 2, top)
    split = (low <= 1) & (top >= 2)

    def chi_arrived(k, slot):
        remote(
            part.at[0], chi_in.at[k, slot], chi_send.at[0, 0], chi_recv.at[k, slot], b, z_right
        ).wait_recv()

    for k in range(blocks):
        @pl.when((b != k) | (owner != z))
        def _():
            chi_arrived(k, 0)

        @pl.when(split & ((b != k) | (low != z)))
        def _():
            chi_arrived(k, 1)
    total = chi_in[0, 0] + chi_in[1, 0] + chi_in[2, 0] + chi_in[3, 0]
    out_ref[...] = total[:, : out_ref.shape[1]] * scale

    @pl.when(split)
    def _():
        rest = chi_in[0, 1] + chi_in[1, 1] + chi_in[2, 1] + chi_in[3, 1]
        out_ref[...] = (total + rest)[:, : out_ref.shape[1]] * scale

    virt_up.wait_send()
    virt_down.wait_send()
    for copy in flag_copies:
        copy.wait_send()
    for k in range(CHUNKS):
        bas_copy(b, k, y_send, y_recv, across, True).wait_send()
        bas_copy(b, k, core_send, core_recv, core, True).wait_send()
        bas_copy(across, k, fwd_send, fwd_recv, core).wait_send()
    for at, f, first in (
        (0, 0, True), (1, 0, False), (2, 0, False), (1, 1, True), (2, 1, False), (0, 2, True),
        (3, 3, True), (2, 4, True), (1, 4, False), (3, 5, True), (1, 5, False),
    ):
        @pl.when(z == at)
        def _():
            for k in range(CHUNKS):
                flow(f, k, first).wait_send()

    @pl.when(b != z)
    def _():
        own.wait_send()

    def shared(other, slot):
        near = slot == 0
        chi_copy(other, not near, slot).wait_send()

        @pl.when(b != other)
        def _():
            chi_copy(other, near, slot).wait_send()

    for at, other, slot in (
        (0, 2, 1), (0, 3, 1), (1, 0, 0), (1, 2, 1), (1, 3, 1),
        (2, 0, 0), (2, 1, 0), (2, 3, 0), (3, 0, 0), (3, 1, 0),
    ):
        @pl.when(z == at)
        def _():
            shared(other, slot)


def one_kernel(three_index, screen, green_occ, green_virt):
    aux_rows, width, band = three_index.shape
    nbasis = green_virt.shape[1]
    scale = -2.0 / math.sqrt(3 * width * width)
    bf16, f32 = jnp.bfloat16, jnp.float32
    dma = pltpu.SemaphoreType.DMA
    return pl.pallas_call(
        functools.partial(kernel, scale),
        out_shape=jax.ShapeDtypeStruct((aux_rows, aux_rows), f32),
        in_specs=[pl.BlockSpec(memory_space=pl.ANY)] * 4,
        out_specs=pl.BlockSpec(memory_space=pltpu.VMEM),
        scratch_shapes=[
            pltpu.VMEM((4, aux_rows, width, band), bf16),
            pltpu.VMEM((4, aux_rows, width, band), bf16),
            pltpu.VMEM((2, aux_rows, 3 * width // 8, band), bf16),
            pltpu.VMEM((aux_rows, width, band), bf16),
            pltpu.VMEM((aux_rows // CHUNKS, nbasis, band), bf16),
            pltpu.VMEM((width, nbasis), bf16),
            pltpu.VMEM((3, width, nbasis), bf16),
            pltpu.VMEM((nbasis + 2 * width, band), bf16),
            pltpu.SMEM((1, 3), jnp.int32),
            pltpu.VMEM((4, 8, band), f32),
            pltpu.VMEM((4, aux_rows, 128), f32),
            pltpu.VMEM((4, aux_rows, 128), f32),
            pltpu.VMEM((4, 2, aux_rows, 128), f32),
        ]
        + [dma((CHUNKS,))] * 6
        + [dma((2,))] * 2
        + [dma((6, CHUNKS))] * 2
        + [dma((4, 2)), dma((4, 2)), dma((3,)), dma((3,)), dma((4,))],
        compiler_params=pltpu.CompilerParams(
            collective_id=0, has_side_effects=True, vmem_limit_bytes=56 * 1024 * 1024
        ),
    )(three_index, screen, green_occ, green_virt)


def padded_2(x, sides, width):
    for axis, dim in sides:
        count, length = (lax.axis_size(axis), x.shape[dim])
        up = [(i, (i + 1) % count) for i in range(count)]
        down = [(j, i) for i, j in up]
        last = lax.slice_in_dim(x, length - width, length, axis=dim)
        initial = lax.slice_in_dim(x, 0, width, axis=dim)
        before = lax.ppermute(last, axis, up)
        after = lax.ppermute(initial, axis, down)
        x = jnp.concatenate([before, x, after], axis=dim)
    return x


def body(three_index, screen, green_occ, green_virt):
    width = green_virt.shape[0]
    aux_rows = three_index.shape[0]
    nbasis = green_virt.shape[1]
    screen_flags = screen[0].astype(jnp.bfloat16)
    masked = (
        three_index.reshape(aux_rows, width, 3, width) * screen_flags[None, None, :, None]
    ).reshape(aux_rows, width, 3 * width)
    virt_rows = padded_2(green_virt, (("bas", 0),), width)
    half = jnp.dot(
        masked.reshape(aux_rows * width, 3 * width), virt_rows, preferred_element_type=jnp.float32
    )
    half = half.astype(jnp.bfloat16).reshape(aux_rows, width, nbasis)
    padded = jnp.concatenate([half[:, :, nbasis - width :], half, half[:, :, :width]], 2)

    def one_block(offset):
        begin = offset * width
        occ_cols = lax.dynamic_slice_in_dim(green_occ, begin, width, 1)
        virt_band = lax.dynamic_slice_in_dim(padded, begin, 3 * width, 2)
        return jnp.einsum("lm,alc->mac", occ_cols, virt_band, preferred_element_type=jnp.float32)

    parts_out = lax.map(
        one_block, jnp.arange(lax.axis_size("bas") * width // width, dtype=jnp.int32)
    )
    summed = lax.psum_scatter(
        parts_out.reshape(lax.axis_size("bas") * width, aux_rows, 3 * width),
        "bas",
        scatter_dimension=0,
        tiled=True,
    )
    middle = jnp.transpose(summed, (1, 0, 2)).astype(jnp.bfloat16)
    partial_chi = jnp.einsum(
        "pmc,qmc->pq",
        masked,
        lax.all_gather(middle, "aux", axis=0, tiled=True),
        preferred_element_type=jnp.float32,
    )
    summed_chi = lax.psum_scatter(partial_chi, "bas", scatter_dimension=1, tiled=True)
    return summed_chi * (-2.0 / math.sqrt(3 * width * width))


def solution(mesh):
    in_specs = (
        P(("grp", "aux"), "bas", None),
        P(("grp", "bas"), None),
        P(("grp", "bas"), None),
        P(("grp", "bas"), None),
    )
    out_specs = P(("grp", "aux"), "bas")
    fits = mesh.shape["bas"] == 4 and mesh.shape["aux"] == 4
    return jax.shard_map(one_kernel if fits else body, mesh=mesh, in_specs=in_specs, out_specs=out_specs, check_vma=False)
```

```python
import functools
import math

import jax
import jax.numpy as jnp
from jax import lax
from jax.experimental import pallas as pl
from jax.experimental.pallas import tpu as pltpu
from jax.sharding import PartitionSpec as P

MESH = pl.DeviceIdType.MESH
CHUNKS = 4


def kernel(
    scale,
    three_ref, screen_ref, occ_hbm, virt_hbm, out_ref,
    ball, zall, mall, mid, half, occ_ref, virt_band, virt_ext, flags_ref, flag_rows, part, part_t, chi_in,
    y_send, y_recv, core_send, core_recv, fwd_send, fwd_recv,
    virt_send, virt_recv, z_send, z_recv, chi_send, chi_recv, flag_send, flag_recv, local_sem,
):
    aux_rows, width, band = three_ref.shape
    blocks = 4
    step = aux_rows // CHUNKS
    late = 3 * width // 8
    early = width - late
    g, b, z = lax.axis_index("grp"), lax.axis_index("bas"), lax.axis_index("aux")
    core = b + 1 - 2 * lax.rem(b, 2)
    across = lax.rem(b + 2, blocks)
    corner = blocks - 1 - b
    above, below = lax.rem(b + 1, blocks), lax.rem(b + blocks - 1, blocks)

    barrier = pltpu.get_barrier_semaphore()
    for k in range(1, 16):
        other = lax.rem(b * 4 + z + k, 16)
        pl.semaphore_signal(
            barrier, inc=1, device_id=(g, other // 4, lax.rem(other, 4)), device_id_type=MESH
        )

    own_copies = [
        pltpu.make_async_copy(screen_ref, flags_ref, local_sem.at[0]),
        pltpu.make_async_copy(three_ref, ball.at[b], local_sem.at[1]),
        pltpu.make_async_copy(virt_hbm, virt_band.at[1], local_sem.at[2]),
        pltpu.make_async_copy(occ_hbm, occ_ref, local_sem.at[3]),
    ]
    for copy in own_copies:
        copy.start()
    own_copies[0].wait()
    lane = lax.broadcasted_iota(jnp.int32, (8, band), 1)
    flags = [flags_ref[0, w].astype(jnp.float32) for w in range(3)]
    flag_rows[b] = jnp.where(lane < width, flags[0], jnp.where(lane < 2 * width, flags[1], flags[2]))
    pl.semaphore_wait(barrier, 15)

    def remote(src, dst, send, recv, bas, aux):
        return pltpu.make_async_remote_copy(
            src_ref=src, dst_ref=dst, send_sem=send, recv_sem=recv,
            device_id=(g, bas, aux), device_id_type=MESH,
        )

    def bas_copy(block, k, sends, recvs, to, first=False):
        rows = ball.at[block, pl.ds(k * step, step)]
        src = three_ref.at[pl.ds(k * step, step)] if first else rows
        return remote(src, rows, sends.at[k], recvs.at[k], to, z)

    z_right, z_left = lax.rem(z + 1, 4), lax.rem(z + 3, 4)

    def flow(f, k, first):
        aux = pl.ds(k * step, step)
        if f >= 4:
            dst = mall.at[f - 4, aux]
            src = mid.at[aux, pl.ds(early, late)] if first else dst
        else:
            rows = (pl.ds(0, early), pl.ds(0, early), pl.ds(early, late), pl.ds(0, width))[f]
            dst = zall.at[(0, 1, 0, 3)[f], aux, rows]
            src = three_ref.at[aux, rows] if first else dst
        to = z_right if f < 3 else lax.rem(z + 2, 4) if f == 5 and first else z_left
        return remote(src, dst, z_send.at[f, k], z_recv.at[f, k], b, to)

    def relay(at, f, k):
        @pl.when(z == at)
        def _():
            flow(f, k, False).wait_recv()
            flow(f, k, False).start()

    def arrived(f):
        for k in range(CHUNKS):
            flow(f, k, False).wait_recv()

    virt_up = remote(virt_hbm, virt_band.at[0], virt_send.at[0], virt_recv.at[0], above, z)
    virt_down = remote(virt_hbm, virt_band.at[2], virt_send.at[1], virt_recv.at[1], below, z)
    for at, f in ((0, 0), (1, 1), (3, 3)):
        @pl.when(z == at)
        def _():
            for k in range(CHUNKS):
                flow(f, k, True).start()
    virt_up.start()
    virt_down.start()
    flag_copies = [
        remote(flag_rows.at[b], flag_rows.at[b], flag_send.at[n], flag_recv.at[n], to, z)
        for n, to in enumerate((core, across, corner))
    ]
    for copy in flag_copies:
        copy.start()
    for k in range(CHUNKS):
        bas_copy(b, k, y_send, y_recv, across, True).start()
        bas_copy(b, k, core_send, core_recv, core, True).start()

    @pl.when(z == 0)
    def _():
        for k in range(CHUNKS):
            flow(2, k, True).start()

    for copy in own_copies[1:]:
        copy.wait()
    virt_up.wait_recv()
    virt_down.wait_recv()
    for w in range(3):
        turned = virt_band[w].astype(jnp.float32).T.astype(jnp.bfloat16)
        cols = pl.ds(w * width, width)
        virt_ext[pl.ds(width, blocks * width), cols] = turned
        virt_ext[pl.ds(0, width), cols] = turned[(blocks - 1) * width :]
        virt_ext[pl.ds((blocks + 1) * width, width), cols] = turned[:width]
    for n, sender in enumerate((core, across, corner)):
        remote(
            flag_rows.at[b], flag_rows.at[sender], flag_send.at[n], flag_recv.at[n], core, z
        ).wait_recv()
    flag_row = flag_rows[b, :1]
    part[z] = jnp.zeros((aux_rows, 128), jnp.float32)

    chi_lane = lax.broadcasted_iota(jnp.int32, (aux_rows, 128), 1)

    def two_columns(three, middle, t, acc):
        count = three.shape[1]
        row = lax.broadcasted_iota(jnp.int32, (count, 2 * count), 0)
        col = lax.broadcasted_iota(jnp.int32, (count, 2 * count), 1)
        same = jnp.where((col == row) | (col == row + count), 1.0, 0.0).astype(jnp.float32)
        left = lax.broadcasted_iota(jnp.int32, (aux_rows, 2 * count), 1) < count
        rows = three[...].reshape(aux_rows * count, band)
        ours = middle[pl.ds(2 * t, 2)].reshape(2 * count, band)
        prod = lax.dot_general(
            rows, ours, (((1,), (1,)), ((), ())), preferred_element_type=jnp.float32
        )
        kept = jnp.sum(prod.reshape(aux_rows, count, 2 * count) * same[None], axis=1)
        first = jnp.sum(jnp.where(left, kept, 0.0), axis=1, keepdims=True)
        second = jnp.sum(jnp.where(left, 0.0, kept), axis=1, keepdims=True)
        return jnp.where(chi_lane == 2 * t, first, jnp.where(chi_lane == 2 * t + 1, second, acc))

    nothing = jnp.zeros((aux_rows, 128), jnp.float32)

    def pair(three, middle):
        return lax.fori_loop(
            0, aux_rows // 2, lambda t, acc: two_columns(three, middle, t, acc), nothing
        )

    def middle_of(k):
        bas_copy(core, k, core_send, core_recv, core).wait_recv()
        bas_copy(corner, k, fwd_send, fwd_recv, core).wait_recv()

        def one_block(l, carry):
            rows = pl.ds(pl.multiple_of(l * width, width), width)
            virt = virt_ext[pl.ds(pl.multiple_of(l * width, width), band), :]
            three = ball[l, pl.ds(k * step, step)].reshape(step * width, band)
            three = three * flag_rows[l, :1].astype(jnp.bfloat16)
            value = jnp.dot(three, virt, preferred_element_type=jnp.float32)
            half[:, rows, :] = value.astype(jnp.bfloat16).reshape(step, width, band)
            return carry

        lax.fori_loop(0, blocks, one_block, 0)
        for q in range(step):
            value = jnp.dot(occ_ref[...], half[q], preferred_element_type=jnp.float32)
            mid[k * step + q] = (value * flag_row).astype(jnp.bfloat16)
        for at, f in ((2, 4), (3, 5)):
            @pl.when(z == at)
            def _():
                flow(f, k, True).start()

    def own_columns(k):
        for t in range(k * step // 2, (k + 1) * step // 2):
            part[z] = two_columns(ball.at[b], mid, t, part[z])

    upward = {
        1: [(0, k) for k in range(CHUNKS)] + [None] * CHUNKS,
        2: [(1, k) for k in range(CHUNKS)] + [(0, k) for k in range(CHUNKS)],
    }

    def pass_up(n):
        for at, chunks in upward.items():
            if chunks[n] is not None:
                relay(at, *chunks[n])

    for k in range(CHUNKS):
        pass_up(2 * k)
        bas_copy(across, k, y_send, y_recv, across).wait_recv()
        bas_copy(across, k, fwd_send, fwd_recv, core).start()
        pass_up(2 * k + 1)
        middle_of(k)
        if k:
            relay(1, 4, k - 1)
            relay(1, 5, k - 1)
        own_columns(k)

    def chi_copy(other, turned, slot):
        src = part_t.at[other] if turned else part.at[other]
        to = (z, other) if turned == bool(slot) else (other, z)
        return remote(
            src, chi_in.at[b, slot], chi_send.at[other, int(turned)], chi_recv.at[b, slot], *to
        )

    def share(other, slot, acc):
        part[other] = acc
        full = jnp.concatenate([acc, jnp.zeros((128 - aux_rows, 128), jnp.float32)], 0)
        part_t[other] = full.T[:aux_rows]
        near = slot == 0
        chi_copy(other, not near, slot).start()

        @pl.when(b == other)
        def _():
            chi_in[b, slot] = part_t[other] if near else part[other]

        @pl.when(b != other)
        def _():
            chi_copy(other, near, slot).start()

    own = remote(part.at[z], chi_in.at[b, 0], chi_send.at[z, 0], chi_recv.at[b, 0], z, z)

    @pl.when(b == z)
    def _():
        chi_in[b, 0] = part[z]

    @pl.when(b != z)
    def _():
        own.start()

    relay(1, 4, CHUNKS - 1)
    relay(1, 5, CHUNKS - 1)

    @pl.when(z == 1)
    def _():
        arrived(2)
        share(0, 0, pair(zall.at[0], mid))

    @pl.when(z == 2)
    def _():
        arrived(3)
        share(3, 0, pair(zall.at[3], mid))

    @pl.when(z >= 2)
    def _():
        for i in (1, 0):
            @pl.when(z == 3)
            def _():
                arrived(i)
            share(i, 0, pair(zall.at[i, :, pl.ds(0, early)], mid.at[:, pl.ds(0, early)]))

    @pl.when(z <= 1)
    def _():
        acc = {2: nothing, 3: nothing}
        for i, k in ((2, 0), (3, 0), (2, 1), (3, 1), (2, 2), (3, 2), (2, 3), (3, 3)):
            @pl.when(z == 0)
            def _():
                flow(i + 2, k, False).wait_recv()
            for t in range(k * step // 2, (k + 1) * step // 2):
                acc[i] = two_columns(ball.at[b, :, pl.ds(early, late)], mall.at[i - 2], t, acc[i])
            if k == CHUNKS - 1:
                share(i, 1, acc[i])

    top = jnp.maximum(b, z)
    low = jnp.minimum(b, z)
    owner = jnp.where((top == 3) & (low == 2), 2, top)
    split = (low <= 1) & (top >= 2)

    def chi_arrived(k, slot):
        remote(
            part.at[0], chi_in.at[k, slot], chi_send.at[0, 0], chi_recv.at[k, slot], b, z_right
        ).wait_recv()

    for k in range(blocks):
        @pl.when((b != k) | (owner != z))
        def _():
            chi_arrived(k, 0)

        @pl.when(split & ((b != k) | (low != z)))
        def _():
            chi_arrived(k, 1)
    total = chi_in[0, 0] + chi_in[1, 0] + chi_in[2, 0] + chi_in[3, 0]
    out_ref[...] = total[:, : out_ref.shape[1]] * scale

    @pl.when(split)
    def _():
        rest = chi_in[0, 1] + chi_in[1, 1] + chi_in[2, 1] + chi_in[3, 1]
        out_ref[...] = (total + rest)[:, : out_ref.shape[1]] * scale

    virt_up.wait_send()
    virt_down.wait_send()
    for copy in flag_copies:
        copy.wait_send()
    for k in range(CHUNKS):
        bas_copy(b, k, y_send, y_recv, across, True).wait_send()
        bas_copy(b, k, core_send, core_recv, core, True).wait_send()
        bas_copy(across, k, fwd_send, fwd_recv, core).wait_send()
    for at, f, first in (
        (0, 0, True), (1, 0, False), (2, 0, False), (1, 1, True), (2, 1, False), (0, 2, True),
        (3, 3, True), (2, 4, True), (1, 4, False), (3, 5, True), (1, 5, False),
    ):
        @pl.when(z == at)
        def _():
            for k in range(CHUNKS):
                flow(f, k, first).wait_send()

    @pl.when(b != z)
    def _():
        own.wait_send()

    def shared(other, slot):
        near = slot == 0
        chi_copy(other, not near, slot).wait_send()

        @pl.when(b != other)
        def _():
            chi_copy(other, near, slot).wait_send()

    for at, other, slot in (
        (0, 2, 1), (0, 3, 1), (1, 0, 0), (1, 2, 1), (1, 3, 1),
        (2, 0, 0), (2, 1, 0), (2, 3, 0), (3, 0, 0), (3, 1, 0),
    ):
        @pl.when(z == at)
        def _():
            shared(other, slot)


def one_kernel(three_index, screen, green_occ, green_virt):
    aux_rows, width, band = three_index.shape
    nbasis = green_virt.shape[1]
    scale = -2.0 / math.sqrt(3 * width * width)
    bf16, f32 = jnp.bfloat16, jnp.float32
    dma = pltpu.SemaphoreType.DMA
    return pl.pallas_call(
        functools.partial(kernel, scale),
        out_shape=jax.ShapeDtypeStruct((aux_rows, aux_rows), f32),
        in_specs=[pl.BlockSpec(memory_space=pl.ANY)] * 4,
        out_specs=pl.BlockSpec(memory_space=pltpu.VMEM),
        scratch_shapes=[
            pltpu.VMEM((4, aux_rows, width, band), bf16),
            pltpu.VMEM((4, aux_rows, width, band), bf16),
            pltpu.VMEM((2, aux_rows, 3 * width // 8, band), bf16),
            pltpu.VMEM((aux_rows, width, band), bf16),
            pltpu.VMEM((aux_rows // CHUNKS, nbasis, band), bf16),
            pltpu.VMEM((width, nbasis), bf16),
            pltpu.VMEM((3, width, nbasis), bf16),
            pltpu.VMEM((nbasis + 2 * width, band), bf16),
            pltpu.SMEM((1, 3), jnp.int32),
            pltpu.VMEM((4, 8, band), f32),
            pltpu.VMEM((4, aux_rows, 128), f32),
            pltpu.VMEM((4, aux_rows, 128), f32),
            pltpu.VMEM((4, 2, aux_rows, 128), f32),
        ]
        + [dma((CHUNKS,))] * 6
        + [dma((2,))] * 2
        + [dma((6, CHUNKS))] * 2
        + [dma((4, 2)), dma((4, 2)), dma((3,)), dma((3,)), dma((4,))],
        compiler_params=pltpu.CompilerParams(
            collective_id=0, has_side_effects=True, vmem_limit_bytes=56 * 1024 * 1024
        ),
    )(three_index, screen, green_occ, green_virt)


def padded_2(x, sides, width):
    for axis, dim in sides:
        count, length = (lax.axis_size(axis), x.shape[dim])
        up = [(i, (i + 1) % count) for i in range(count)]
        down = [(j, i) for i, j in up]
        last = lax.slice_in_dim(x, length - width, length, axis=dim)
        initial = lax.slice_in_dim(x, 0, width, axis=dim)
        before = lax.ppermute(last, axis, up)
        after = lax.ppermute(initial, axis, down)
        x = jnp.concatenate([before, x, after], axis=dim)
    return x


def body(three_index, screen, green_occ, green_virt):
    width = green_virt.shape[0]
    aux_rows = three_index.shape[0]
    nbasis = green_virt.shape[1]
    screen_flags = screen[0].astype(jnp.bfloat16)
    masked = (
        three_index.reshape(aux_rows, width, 3, width) * screen_flags[None, None, :, None]
    ).reshape(aux_rows, width, 3 * width)
    virt_rows = padded_2(green_virt, (("bas", 0),), width)
    half = jnp.dot(
        masked.reshape(aux_rows * width, 3 * width), virt_rows, preferred_element_type=jnp.float32
    )
    half = half.astype(jnp.bfloat16).reshape(aux_rows, width, nbasis)
    padded = jnp.concatenate([half[:, :, nbasis - width :], half, half[:, :, :width]], 2)

    def one_block(offset):
        begin = offset * width
        occ_cols = lax.dynamic_slice_in_dim(green_occ, begin, width, 1)
        virt_band = lax.dynamic_slice_in_dim(padded, begin, 3 * width, 2)
        return jnp.einsum("lm,alc->mac", occ_cols, virt_band, preferred_element_type=jnp.float32)

    parts_out = lax.map(
        one_block, jnp.arange(lax.axis_size("bas") * width // width, dtype=jnp.int32)
    )
    summed = lax.psum_scatter(
        parts_out.reshape(lax.axis_size("bas") * width, aux_rows, 3 * width),
        "bas",
        scatter_dimension=0,
        tiled=True,
    )
    middle = jnp.transpose(summed, (1, 0, 2)).astype(jnp.bfloat16)
    partial_chi = jnp.einsum(
        "pmc,qmc->pq",
        masked,
        lax.all_gather(middle, "aux", axis=0, tiled=True),
        preferred_element_type=jnp.float32,
    )
    summed_chi = lax.psum_scatter(partial_chi, "bas", scatter_dimension=1, tiled=True)
    return summed_chi * (-2.0 / math.sqrt(3 * width * width))


def solution(mesh):
    in_specs = (
        P(("grp", "aux"), "bas", None),
        P(("grp", "bas"), None),
        P(("grp", "bas"), None),
        P(("grp", "bas"), None),
    )
    out_specs = P(("grp", "aux"), "bas")
    fits = mesh.shape["bas"] == 4 and mesh.shape["aux"] == 4
    return jax.shard_map(one_kernel if fits else body, mesh=mesh, in_specs=in_specs, out_specs=out_specs, check_vma=False)
```
